32 devices in a mesh: feat: 16 (over z, x, core), tok: 2 (over y).
Axes of the slice: x: 2, y: 2, z: 4, core: 2. Of those that a mesh axis runs over, the one named last changes fastest.
Arguments:
- acts_in: bfloat16 [768, 2, 2304], P(('tok', 'feat')), may hold values from -6 to 6
- targets: bfloat16 [768, 2, 2304], P(('tok', 'feat')), may hold values from -6 to 6
- enc_weight: bfloat16 [2, 2304, 16384], P(None, None, 'feat'), may hold values from -0.125 to 0.125
- enc_bias: float32 [2, 16384], P(None, 'feat'), may hold values from -3 to 3
- dec_weight: bfloat16 [3, 16384, 2304], P(None, 'feat'), may hold values from -0.046875 to 0.046875
Outputs:
- grad_enc: bfloat16 [2, 2304, 16384], P(None, 'tok', 'feat')
- grad_enc_bias: float32 [2, 16384], P(None, ('feat', 'tok'))
- grad_dec: bfloat16 [3, 16384, 2304], P(None, ('feat', 'tok'))
The draws below stay inside these ranges and needn't reach their ends.
All inputs are finite; a program needn't handle non-finite values.
Results may differ from the reference program's by a relative error of at most 0.02.
Values may be sent and summed in bfloat16 or wider, within the bound.
No kernel may reach another device: no remote copies, remote signals or barrier semaphores. Data moves between devices by JAX's collectives and lax.ppermute only.
A program may use at most 128 MiB of HBM per device.

```python
import math
import jax
import jax.numpy as jnp
from jax import lax

D = 2304
F = 16384
L = 2
TOK_DEV = 384
PAIRS = 3
TOKENS = 768


def level_of(key, extent, shards, smallest, high):
    def one(dim, blocks):
        draws = jax.random.uniform(jax.random.fold_in(jax.random.fold_in(key, 6), dim), (blocks,), jnp.float32, smallest / len(shards), high / len(shards))
        return jnp.repeat(jnp.exp(draws), extent[dim] // blocks).reshape((-1,) + (1,) * (len(extent) - dim - 1))

    level = one(*shards[0])
    for cut in shards[1:]:
        level = level * one(*cut)
    return level


def centred(stream_key, extent, scale, most, split=(), kind=jnp.bfloat16):
    loudness = level_of(stream_key, extent, split, -0.22, 0.18) if split else 1.0
    result = jax.random.normal(stream_key, extent, jnp.float32) * scale * loudness
    return jnp.minimum(jnp.maximum(result, -most), most).astype(kind)


def setup_inputs(seed: int = 0) -> dict:
    keys = jax.random.split(jax.random.key(seed), 6)
    acts_in = centred(keys[0], (TOKENS, L, D), 1.0, 6.0, ((0, 32),))
    targets = centred(keys[1], (TOKENS, L, D), 1.0, 6.0, ((0, 32),))
    enc_weight = centred(keys[2], (L, D, F), D ** -0.5, 0.125, ((2, 16),))
    enc_bias = centred(keys[3], (L, F), 0.5, 3.0, ((1, 16),), jnp.float32)
    dec_weight = centred(keys[4], (PAIRS, F, D), F ** -0.5, 0.046875, ((1, 16),))
    return {"acts_in": acts_in, "targets": targets, "enc_weight": enc_weight, "enc_bias": enc_bias, "dec_weight": dec_weight}


def pair_slot(source, target, layers):
    return sum((layers - k for k in range(source))) + (target - source)

def reference(acts_in, targets, enc_weight, enc_bias, dec_weight):
    layers = L
    preacts = []
    coded = []
    for source in range(layers):
        value = jnp.dot(acts_in[:, source, :], enc_weight[source], preferred_element_type=jnp.float32) + enc_bias[source]
        preacts.append(value)
        coded.append((0.5 * jnp.maximum(value, 0.0) ** 2).astype(jnp.bfloat16))
    rebuilt = []
    for target in range(layers):
        total = jnp.zeros((acts_in.shape[0], D), jnp.float32)
        for source in range(target + 1):
            total = total + jnp.dot(coded[source], dec_weight[pair_slot(source, target, layers)], preferred_element_type=jnp.float32)
        rebuilt.append(total)
    errors = (jnp.stack(rebuilt, axis=1) - targets.astype(jnp.float32)).astype(jnp.bfloat16)
    dpreacts = []
    for source in range(layers):
        dcoded = jnp.zeros((acts_in.shape[0], F), jnp.float32)
        for target in range(source, layers):
            dcoded = dcoded + lax.dot_general(errors[:, target, :], dec_weight[pair_slot(source, target, layers)], (((1,), (1,)), ((), ())), preferred_element_type=jnp.float32)
        dpreacts.append((dcoded * jnp.maximum(preacts[source], 0.0)).astype(jnp.bfloat16))
    loss_scale = 1.0 / math.sqrt(TOKENS)
    groups = TOKENS // TOK_DEV
    inputs_g = acts_in.reshape(groups, TOK_DEV, layers, D)
    errors_g = errors.reshape(groups, TOK_DEV, layers, D)
    coded_g = jnp.stack(coded, axis=0).reshape(layers, groups, TOK_DEV, F).transpose(1, 0, 2, 3)
    dpre_g = jnp.stack(dpreacts, axis=0).reshape(layers, groups, TOK_DEV, F).transpose(1, 0, 2, 3)

    def step(carry, group):
        enc_sum, bias_sum, dec_sum = carry
        inputs, errs, codes, dpres = group
        enc_parts = []
        bias_parts = []
        for source in range(layers):
            part = jnp.dot(inputs[:, source, :].T, dpres[source], preferred_element_type=jnp.float32) * loss_scale
            enc_parts.append(part.astype(jnp.bfloat16).astype(jnp.float32))
            bias_part = lax.optimization_barrier(jnp.sum(dpres[source].astype(jnp.float32), axis=0)) * loss_scale
            bias_parts.append(bias_part.astype(jnp.bfloat16).astype(jnp.float32))
        dec_parts = []
        for source in range(layers):
            for target in range(source, layers):
                part = jnp.dot(codes[source].T, errs[:, target, :], preferred_element_type=jnp.float32) * loss_scale
                dec_parts.append(part.astype(jnp.bfloat16).astype(jnp.float32))
        return ((enc_sum + jnp.stack(enc_parts), bias_sum + jnp.stack(bias_parts), dec_sum + jnp.stack(dec_parts)), None)
    start = (jnp.zeros((layers, D, F), jnp.float32), jnp.zeros((layers, F), jnp.float32), jnp.zeros((PAIRS, F, D), jnp.float32))
    (enc_sum, bias_sum, dec_sum), _ = lax.scan(step, start, (inputs_g, errors_g, coded_g, dpre_g))
    return (enc_sum.astype(jnp.bfloat16), bias_sum, dec_sum.astype(jnp.bfloat16))
```

```python
import math

import jax
import jax.numpy as jnp
from jax import lax
from jax.sharding import PartitionSpec as P


def pair_slot(source, target, layers):
    return sum((layers - k for k in range(source))) + (target - source)


def swap(value, axis, bits):
    return lax.ppermute(value, axis, [(i, i ^ bits) for i in range(lax.axis_size(axis))])


def rows(value, start, count):
    return lax.slice_in_dim(value, start, start + count, axis=-2)


def dot(a, b, dims):
    return lax.dot_general(a, b, (dims, ((), ())), preferred_element_type=jnp.float32)


def shards(acts_in, targets, enc_weight, enc_bias, dec_weight):
    layers, width, feats = enc_weight.shape
    n = acts_in.shape[0]
    feat, tok = lax.axis_size("feat"), lax.axis_size("tok")
    half = feat // 2
    quart = feat // 4
    tok_rows = n * feat
    scale = 1.0 / math.sqrt(tok_rows * tok)
    me = lax.axis_index("tok")
    own_width, own_feats = width // tok, feats // tok

    def near(value):
        first = [value] + [swap(value, "feat", 4 * k) for k in range(1, quart)]
        return first + [swap(v, "feat", 2) for v in first]

    def both(column):
        return jnp.concatenate([column, swap(column, "feat", 1)], axis=-2)

    def encode(inputs):
        pre = []
        for s in range(layers):
            value = dot(inputs[s], enc_weight[s], ((1,), (0,))) + enc_bias[s]
            pre.append(jnp.maximum(value, 0.0))
        return pre, [(0.5 * p * p).astype(jnp.bfloat16) for p in pre]

    acts = jnp.swapaxes(acts_in, 0, 1)
    column = jnp.concatenate(near(acts), axis=-2)
    inputs = [both(column)]
    pre, coded = [], []
    p, c = encode(inputs[0])
    pre.append(p)
    coded.append(c)

    own = []
    for t in range(layers):
        total = None
        for s in range(t + 1):
            term = dot(c[s], dec_weight[pair_slot(s, t, layers)], ((1,), (0,)))
            total = term if total is None else total + term
        part = total.astype(jnp.bfloat16)
        got = swap(rows(part, half * n, half * n), "feat", 1)
        part = (rows(part, 0, half * n).astype(jnp.float32) + got.astype(jnp.float32)).astype(jnp.bfloat16)
        blocks = []
        for k in reversed(range(quart)):
            got = swap(rows(part, (quart + k) * n, n), "feat", 2)
            block = rows(part, k * n, n).astype(jnp.float32) + got.astype(jnp.float32)
            if k:
                block = swap(block.astype(jnp.bfloat16), "feat", 4 * k).astype(jnp.float32)
            blocks.append(block)
        own.append(sum(blocks[1:], blocks[0]))

    error = jnp.stack(
        [(own[t] - targets[:, t, :].astype(jnp.float32)).astype(jnp.bfloat16) for t in range(layers)]
    )

    for k in range(1, tok):
        inputs.append(both(swap(column, "tok", k)))
        p, c = encode(inputs[-1])
        pre.append(p)
        coded.append(c)

    blocks = near(error)
    errors = [both(jnp.concatenate(blocks, axis=-2))]
    for k in range(1, tok):
        z_part = [swap(b, "tok", k) for b in blocks[:quart]]
        x_part = [swap(b, "tok", k) for b in blocks[quart:quart + quart // 2]]
        x_part += [swap(b, "feat", 2) for b in z_part[quart // 2:]]
        errors.append(both(jnp.concatenate(z_part + x_part, axis=-2)))

    dpre = []
    for g in range(tok):
        group = []
        for s in range(layers):
            total = None
            for t in range(s, layers):
                term = dot(errors[g][t], dec_weight[pair_slot(s, t, layers)], ((1,), (1,)))
                total = term if total is None else total + term
            group.append((total * pre[g][s]).astype(jnp.bfloat16))
        dpre.append(group)

    def whole(parts):
        return jnp.concatenate(parts, axis=0)

    dec_out = []
    for s in range(layers):
        codes = whole([lax.dynamic_slice_in_dim(coded[g][s], me * own_feats, own_feats, axis=1) for g in range(tok)])
        for t in range(s, layers):
            out = dot(codes, whole([errors[g][t] for g in range(tok)]), ((0,), (0,)))
            dec_out.append((out * scale).astype(jnp.bfloat16))
    enc_out, bias_out = [], []
    for s in range(layers):
        seen = whole([lax.dynamic_slice_in_dim(inputs[g][s], me * own_width, own_width, axis=1) for g in range(tok)])
        grads = whole([dpre[g][s] for g in range(tok)])
        enc_out.append((dot(seen, grads, ((0,), (0,))) * scale).astype(jnp.bfloat16))
        mine = lax.dynamic_slice_in_dim(grads, me * own_feats, own_feats, axis=1)
        bias_out.append(jnp.sum(mine.astype(jnp.float32), axis=0) * scale)
    return jnp.stack(enc_out), jnp.stack(bias_out), jnp.stack(dec_out)


def solution(mesh):
    return jax.shard_map(
        shards,
        mesh=mesh,
        in_specs=(
            P(("tok", "feat"), None, None),
            P(("tok", "feat"), None, None),
            P(None, None, "feat"),
            P(None, "feat"),
            P(None, "feat", None),
        ),
        out_specs=(
            P(None, "tok", "feat"),
            P(None, ("feat", "tok")),
            P(None, ("feat", "tok"), None),
        ),
        check_vma=False,
    )
```

```python
import functools
import math

import jax
import jax.numpy as jnp
from jax import lax
from jax.experimental import pallas as pl
from jax.experimental.pallas import tpu as pltpu
from jax.sharding import PartitionSpec as P

MIB = 1 << 20


def pair_slot(source, target, layers):
    return sum((layers - k for k in range(source))) + (target - source)


def swap(value, axis, bits):
    return lax.ppermute(value, axis, [(i, i ^ bits) for i in range(lax.axis_size(axis))])


def cat(parts):
    return parts[0] if len(parts) == 1 else jnp.concatenate(parts, axis=0)


def dot(a, b, dims):
    return lax.dot_general(a, b, (dims, ((), ())), preferred_element_type=jnp.float32)


def piece(size, most):
    for c in range(most - most % 128, 0, -128):
        if size % c == 0:
            return c
    return size


def share(parts, own, me):
    if own % 128:
        return [(lax.dynamic_slice_in_dim(p, me[0] * own, own, axis=1), (p.shape[0], own), lambda j, me: (0, 0)) for p in parts]
    return [(p, (p.shape[0], own), lambda j, me: (0, me[0])) for p in parts]


def view(ref, block, index):
    at = []
    for size, most, i in zip(block, ref.shape, index):
        start = i * size
        at.append(slice(None) if size == most else pl.ds(start if isinstance(start, int) else pl.multiple_of(start, size), size))
    return ref.at[tuple(at)]


def inside(count):
    return [pl.BlockSpec(memory_space=pltpu.VMEM)] * count


def local(kernel, name, arrays, outs, after=(), scalars=(), extra=0):
    skip = len(after)
    return pl.pallas_call(
        lambda *refs: kernel(*refs[skip:]),
        name=name,
        out_shape=[pltpu.VMEM(s, d) for s, d in outs],
        in_specs=[pl.BlockSpec(memory_space=pl.ANY)] * skip
        + [pl.BlockSpec(memory_space=pltpu.SMEM)] * len(scalars)
        + inside(len(arrays)),
        out_specs=inside(len(outs)),
        compiler_params=pltpu.CompilerParams(vmem_limit_bytes=4 * MIB + extra),
        cost_estimate=pl.CostEstimate(flops=0, bytes_accessed=0, transcendentals=0),
    )(*after, *scalars, *[pltpu.with_memory_space_constraint(a, pltpu.VMEM) for a in arrays])


def steps_body(kernel, steps, ins, outs, *refs):
    for j in range(steps):
        kernel(*[view(r, b, m(j)) for r, (b, m) in zip(refs, ins + outs)])


def call(kernel, name, steps, ins, outs, flops, scalars=(), resident=False, after=()):
    if resident:
        body = functools.partial(steps_body, kernel, steps, [i[1:] for i in ins], [o[2:] for o in outs])
        return local(body, name, [i[0] for i in ins], [o[:2] for o in outs], after)
    moved = sum(math.prod(a.shape) * a.dtype.itemsize for a, _, _ in ins)
    moved += sum(math.prod(s) * jnp.dtype(d).itemsize for s, d, _, _ in outs)
    return pl.pallas_call(
        kernel,
        name=name,
        out_shape=[jax.ShapeDtypeStruct(s, d) for s, d, _, _ in outs],
        grid_spec=pltpu.PrefetchScalarGridSpec(
            num_scalar_prefetch=len(scalars),
            grid=(steps,),
            in_specs=[pl.BlockSpec(b, m) for _, b, m in ins],
            out_specs=[pl.BlockSpec(b, m) for _, _, b, m in outs],
        ),
        compiler_params=pltpu.CompilerParams(vmem_limit_bytes=32 * MIB),
        cost_estimate=pl.CostEstimate(flops=flops, bytes_accessed=moved, transcendentals=0),
    )(*scalars, *[i[0] for i in ins])


def load_kernel(count, *refs):
    sources, places, sems = refs[:count], refs[count:2 * count], refs[2 * count]
    copies = [pltpu.make_async_copy(sources[i], places[i], sems.at[i]) for i in range(count)]
    for copy in copies:
        copy.start()
    for copy in copies:
        copy.wait()


def load(arrays, after=()):
    count, skip = len(arrays), len(after)
    return pl.pallas_call(
        lambda *refs: load_kernel(count, *refs[skip:]),
        name="load",
        out_shape=[pltpu.VMEM(a.shape, a.dtype) for a in arrays],
        in_specs=[pl.BlockSpec(memory_space=pl.ANY)] * skip + [pl.BlockSpec(memory_space=pltpu.HBM)] * count,
        out_specs=inside(count),
        scratch_shapes=[pltpu.SemaphoreType.DMA((count,))],
        compiler_params=pltpu.CompilerParams(vmem_limit_bytes=MIB),
        cost_estimate=pl.CostEstimate(flops=0, bytes_accessed=0, transcendentals=0),
    )(*after, *[pltpu.with_memory_space_constraint(a, pltpu.HBM) for a in arrays])


def wide(ref):
    return ref[...].astype(jnp.float32)


def join_kernel(groups, *refs):
    ins, outs = refs[:sum(groups)], refs[sum(groups):]
    for count, out in zip(groups, outs):
        out[...] = cat([wide(r) for r in ins[:count]]).astype(out.dtype)
        ins = ins[count:]


def join(lists, after=(), resident=True):
    if not resident:
        return [cat(parts) for parts in lists]
    outs = [((sum(p.shape[0] for p in parts), parts[0].shape[1]), parts[0].dtype) for parts in lists]
    kernel = functools.partial(join_kernel, [len(parts) for parts in lists])
    return local(kernel, "join", [p for parts in lists for p in parts], outs, after)


def pair_kernel(n, keep, got, low, high_rest, high_own):
    part = wide(keep) + wide(got)
    half = part.shape[0] // 2
    low[...] = part[:half]
    high_own[...] = part[half:half + n].astype(high_own.dtype)
    high_rest[...] = part[half + n:].astype(high_rest.dtype)


def line_kernel(n, low, got, *outs):
    part = low[n:] + wide(got)
    for k, out in enumerate(outs):
        out[...] = part[k * n:(k + 1) * n].astype(out.dtype)


def error_kernel(n, low, *refs):
    refs, target, out = refs[:-2], refs[-2], refs[-1]
    value = low[:n]
    for r in refs:
        value = value + wide(r)
    out[...] = (value - wide(target)).astype(out.dtype)


def run(kernel, name, arrays, outs, after, resident):
    if resident:
        return local(kernel, name, arrays, outs, after)
    cells = [Cell(a) for a in arrays] + [Cell(None, d) for _, d in outs]
    kernel(*cells)
    return [c.value for c in cells[len(arrays):]]


class Cell:
    def __init__(self, value, dtype=None):
        self.value, self.dtype = value, dtype

    def __getitem__(self, at):
        return self.value[at]

    def __setitem__(self, at, value):
        self.value = value


def encode_kernel(parts, *refs):
    x = cat([r[...] for r in refs[:parts]])
    w, b, pre, code = refs[parts:]
    value = jnp.maximum(dot(x, w[0], ((1,), (0,))) + b[0], 0.0)
    pre[...] = value
    code[...] = (0.5 * value * value).astype(code.dtype)


def encode(source, parts, weight, bias, resident, after=()):
    _, width, feats = weight.shape
    m = sum(p.shape[0] for p in parts)
    c = piece(feats, 256)
    ins = [(p, p.shape, lambda j: (0, 0)) for p in parts]
    ins.append((weight, (1, width, c), lambda j: (source, 0, j)))
    ins.append((bias, (1, 1, c), lambda j: (source, 0, j)))
    outs = [((m, feats), d, (m, c), lambda j: (0, j)) for d in (jnp.float32, jnp.bfloat16)]
    return call(
        functools.partial(encode_kernel, len(parts)), "encode", feats // c, ins, outs, 2 * m * width * feats, (), resident, after
    )


def decode_kernel(sources, *refs):
    total = None
    for s in range(sources):
        term = dot(refs[s][...], refs[sources + s][0], ((1,), (0,)))
        total = term if total is None else total + term
    keep, give = refs[2 * sources:]
    half = keep.shape[0]
    keep[...] = total[:half].astype(keep.dtype)
    give[...] = total[half:].astype(give.dtype)


def decode(target, codes, weight, layers, resident, after=()):
    _, feats, width = weight.shape
    m = codes[0].shape[0]
    c = piece(width, 768)
    used = codes[: target + 1]
    ins = [(a, a.shape, lambda j: (0, 0)) for a in used]
    for s in range(target + 1):
        slot = pair_slot(s, target, layers)
        ins.append((weight, (1, feats, c), lambda j, slot=slot: (slot, 0, j)))
    outs = [((m // 2, width), jnp.bfloat16, (m // 2, c), lambda j: (0, j))] * 2
    return call(
        functools.partial(decode_kernel, target + 1),
        "decode",
        width // c,
        ins,
        outs,
        2 * m * width * feats * (target + 1),
        (),
        resident,
        after,
    )


def back_kernel(layers, parts, *refs):
    errors = [cat([r[...] for r in refs[t * parts:(t + 1) * parts]]) for t in range(layers)]
    refs = refs[layers * parts:]
    pre, refs = refs[:layers], refs[layers:]
    pairs = layers * (layers + 1) // 2
    weight, refs = refs[:pairs], refs[pairs:]
    out, total = refs[:layers], refs[layers]
    for s in range(layers):
        value = None
        for t in range(s, layers):
            term = dot(errors[t], weight[pair_slot(s, t, layers)][0], ((1,), (1,)))
            value = term if value is None else value + term
        value = (value * pre[s][...]).astype(out[s].dtype)
        out[s][...] = value
        total[s] = jnp.sum(value.astype(jnp.float32), axis=0, keepdims=True)


def back(errors, pre, weight, layers, resident, after=()):
    pairs, feats, width = weight.shape
    m = pre[0].shape[0]
    c = piece(feats, 256)
    ins = [(e, e.shape, lambda j: (0, 0)) for t in range(layers) for e in errors[t]]
    ins += [(p, (m, c), lambda j: (0, j)) for p in pre]
    ins += [(weight, (1, c, width), lambda j, k=k: (k, j, 0)) for k in range(pairs)]
    outs = [((m, feats), jnp.bfloat16, (m, c), lambda j: (0, j))] * layers
    outs.append(((layers, 1, feats), jnp.float32, (layers, 1, c), lambda j: (0, 0, j)))
    got = call(
        functools.partial(back_kernel, layers, len(errors[0])),
        "back",
        feats // c,
        ins,
        outs,
        2 * m * width * feats * pairs,
        (),
        resident,
        after,
    )
    return got[:layers], got[layers]


def dec_kernel(layers, scale, counts, me, *refs):
    a, b = counts
    codes = [cat([r[...] for r in refs[s * a:(s + 1) * a]]) for s in range(layers)]
    refs = refs[layers * a:]
    errors = [cat([r[...] for r in refs[t * b:(t + 1) * b]]) for t in range(layers)]
    out = refs[layers * b]
    for s in range(layers):
        for t in range(s, layers):
            value = dot(codes[s], errors[t], ((0,), (0,))) * scale
            out[pair_slot(s, t, layers)] = value.astype(out.dtype)


def dec_grads(codes, errors, me, own, scale, layers):
    width = errors[0][0].shape[1]
    pairs = layers * (layers + 1) // 2
    m = sum(p.shape[0] for p in codes[0])
    c = piece(width, 768)
    ins = [i for s in range(layers) for i in share(codes[s], own, me)]
    ins += [(p, (p.shape[0], c), lambda j, me: (0, j)) for t in range(layers) for p in errors[t]]
    outs = [((pairs, own, width), jnp.bfloat16, (pairs, own, c), lambda j, me: (0, 0, j))]
    return call(
        functools.partial(dec_kernel, layers, scale, (len(codes[0]), len(errors[0]))),
        "dec_grads",
        width // c,
        ins,
        outs,
        2 * m * width * own * pairs,
        (me,),
    )[0]


def enc_kernel(layers, scale, counts, me, *refs):
    a, b = counts
    inputs = [cat([r[...] for r in refs[s * a:(s + 1) * a]]) for s in range(layers)]
    refs = refs[layers * a:]
    grads = [cat([r[...] for r in refs[s * b:(s + 1) * b]]) for s in range(layers)]
    out = refs[layers * b]
    for s in range(layers):
        out[s] = (dot(inputs[s], grads[s], ((0,), (0,))) * scale).astype(out.dtype)


def enc_grads(inputs, grads, me, own, scale, layers):
    feats = grads[0][0].shape[1]
    m = sum(p.shape[0] for p in inputs[0])
    c = piece(feats, 256)
    ins = [i for s in range(layers) for i in share(inputs[s], own, me)]
    ins += [(p, (p.shape[0], c), lambda j, me: (0, j)) for s in range(layers) for p in grads[s]]
    outs = [((layers, own, feats), jnp.bfloat16, (layers, own, c), lambda j, me: (0, 0, j))]
    return call(
        functools.partial(enc_kernel, layers, scale, (len(inputs[0]), len(grads[0]))),
        "enc_grads",
        feats // c,
        ins,
        outs,
        2 * m * own * feats * layers,
        (me,),
    )[0]


def grads_body(layers, scale, counts, own, *refs):
    lists = []
    for count in counts:
        lists.append([refs[s * count:(s + 1) * count] for s in range(layers)])
        refs = refs[layers * count:]
    codes, errors, inputs, grads = lists
    sums, refs = refs[:counts[-1]], refs[counts[-1]:]
    dec_out, enc_out, bias_out, dec_held, enc_held, dec_sems, enc_sems = refs
    copies = []
    me = lax.axis_index("tok")

    def mine(size):
        return pl.ds(pl.multiple_of(me * size, 128), size)

    def leave(held, out, sems, slot, left, right):
        width = right.shape[1]
        size = piece(width, 768)
        for j in range(width // size):
            value = dot(left, right[:, j * size:(j + 1) * size], ((0,), (0,)))
            held[slot, :, j * size:(j + 1) * size] = (value * scale).astype(held.dtype)
        copy = pltpu.make_async_copy(held.at[slot], out.at[slot], sems.at[slot])
        copy.start()
        copies.append(copy)

    def columns(parts, size):
        if parts[0].shape[1] == size:
            return cat([p[...] for p in parts])
        return cat([p[:, mine(size)] for p in parts])

    for s in range(layers):
        left = columns(codes[s], own[0])
        for t in range(s, layers):
            right = cat([e[...] for e in errors[t]])
            leave(dec_held, dec_out, dec_sems, pair_slot(s, t, layers), left, right)
    for s in range(layers):
        leave(enc_held, enc_out, enc_sems, s, columns(inputs[s], own[1]), cat([g[...] for g in grads[s]]))
        total = sums[0][s, :, mine(own[0])]
        for more in sums[1:]:
            total = total + more[s, :, mine(own[0])]
        bias_out[pl.ds(s, 1)] = total * scale
    for copy in copies:
        copy.wait()


def all_grads(codes, errors, inputs, grads, sums, own, scale, layers):
    lists = (codes, errors, inputs, grads)
    dec = (layers * (layers + 1) // 2, own[0], errors[0][0].shape[1])
    enc = (layers, own[1], grads[0][0].shape[1])
    arrays = [pltpu.with_memory_space_constraint(p, pltpu.VMEM) for parts in lists for s in parts for p in s]
    arrays += [pltpu.with_memory_space_constraint(p, pltpu.VMEM) for p in sums]
    return pl.pallas_call(
        functools.partial(grads_body, layers, scale, [len(parts[0]) for parts in lists], own),
        name="grads",
        out_shape=[
            jax.ShapeDtypeStruct(dec, jnp.bfloat16),
            jax.ShapeDtypeStruct(enc, jnp.bfloat16),
            jax.ShapeDtypeStruct((layers, own[0]), jnp.float32),
        ],
        in_specs=inside(len(arrays)),
        out_specs=[pl.BlockSpec(memory_space=pltpu.HBM)] * 2 + inside(1),
        scratch_shapes=[
            pltpu.VMEM(dec, jnp.bfloat16),
            pltpu.VMEM(enc, jnp.bfloat16),
            pltpu.SemaphoreType.DMA((dec[0],)),
            pltpu.SemaphoreType.DMA((enc[0],)),
        ],
        compiler_params=pltpu.CompilerParams(vmem_limit_bytes=2 * (math.prod(dec) + math.prod(enc)) + 8 * MIB),
        cost_estimate=pl.CostEstimate(flops=0, bytes_accessed=0, transcendentals=0),
    )(*arrays)


def shards(acts_in, targets, enc_weight, enc_bias, dec_weight):
    layers, width, feats = enc_weight.shape
    n = acts_in.shape[0]
    feat, tok = lax.axis_size("feat"), lax.axis_size("tok")
    scale = 1.0 / math.sqrt(n * feat * tok)
    bias = enc_bias.reshape(layers, 1, feats)
    held = 2 * (math.prod(enc_weight.shape) + math.prod(dec_weight.shape))
    held += 4 * layers * n * feat * tok * (width + 2 * feats)
    resident = held <= 54 * MIB and n % 8 == 0
    line = [4 * k for k in range(1, feat // 4)]
    quart = n * (feat // 4)
    half = 2 * quart
    small = ((n, width), jnp.bfloat16)

    def swap_line(value):
        return [swap(value, "feat", bits) for bits in line]

    own_acts = [acts_in[:, s, :] for s in range(layers)]
    enc_held, dec_held = load([enc_weight, dec_weight]) if resident else (enc_weight, dec_weight)
    found = [swap_line(own_acts[0])]
    across_own = swap(cat(own_acts), "feat", 2)
    columns = []
    pre, codes = [[]], [[]]
    inputs = [[]]
    parts = []
    lines, crossed = [], []
    for s in range(layers):
        lists = [found[s]] + ([[own_acts[s + 1]]] if s + 1 < layers else [])
        made = join(lists, [dec_held] if s == 0 else (), resident)
        lines.append(made[0])
        crossed.append(swap(made[0], "feat", 2))
        if s + 1 < layers:
            found.append(swap_line(made[1]))
    last = ()
    for s in range(layers):
        there = lax.slice_in_dim(across_own, s * n, (s + 1) * n, axis=0)
        gate = found[s + 1] if s + 1 < layers else ()
        column = join([[own_acts[s], lines[s], there, crossed[s]]], gate, resident)[0]
        columns.append(column)
        inputs[0].append([column, swap(column, "feat", 1)])
        p, c = encode(s, inputs[0][s], enc_held, bias, resident, last)
        pre[0].append(p)
        codes[0].append(c)
        keep, give = decode(s, codes[0], dec_held, layers, resident, last)
        got = swap(give, "feat", 1)
        shapes = [((quart, width), jnp.float32), ((quart - n, width), jnp.bfloat16), small]
        low, rest, own = run(functools.partial(pair_kernel, n), "pair", [keep, got], shapes, (), resident)
        parts.append([low, swap(rest, "feat", 2), swap(own, "feat", 2)])
        last = (rest,)

    away = [[swap(columns[s], "tok", g) for s in range(layers)] for g in range(1, tok)]

    for s in range(layers):
        parts[s] += run(functools.partial(line_kernel, n), "line", parts[s][:2], [small] * len(line), (), resident)

    errors = [[] for _ in range(tok)]
    sent, found = [], []
    for t in range(layers):
        got = [swap(v, "feat", bits) for v, bits in zip(parts[t][3:], line)]
        target = targets[:, t, :]
        sent.append(
            run(
                functools.partial(error_kernel, n),
                "error",
                [parts[t][0], parts[t][2]] + got + [target],
                [small],
                found[t - 1] if t else (),
                resident,
            )[0]
        )
        found.append(swap_line(sent[t]))

    last = ()
    for g in range(1, tok):
        inputs.append([])
        pre.append([])
        codes.append([])
        for s in range(layers):
            column = join([[away[g - 1][s]]], sent, resident)[0]
            inputs[g].append([column, swap(column, "feat", 1)])
            p, c = encode(s, inputs[g][s], enc_held, bias, resident, last)
            pre[g].append(p)
            codes[g].append(c)
            last = (c,)

    wholes = []
    for t in range(layers):
        there = swap(sent[t], "feat", 2)
        column, rest = join([[sent[t]] + found[t], found[t]], (), resident)
        crossed = swap(rest, "feat", 2)
        others = [swap(column, "tok", g) for g in range(1, tok)]
        full, side = join([[column, there, crossed], [there, crossed]], others + list(last), resident)
        errors[0].append([full, swap(full, "feat", 1)])
        if t % 2 == 0:
            wholes.append([(o, swap(side, "tok", g)) for g, o in enumerate(others, 1)])
        else:
            wholes.append([(o, swap(o, "feat", 2)) for o in others])
    grads, sums = [], []
    last = ()
    for g in range(tok):
        if g:
            for t in range(layers):
                full = join([list(wholes[t][g - 1])], last, resident)[0]
                errors[g].append([full, swap(full, "feat", 1)])
        d, total = back(errors[g], pre[g], dec_held, layers, resident)
        grads.append(d)
        sums.append(total)
        last = (d[0],)

    def every(parts):
        return [
            [q for g in range(tok) for q in (parts[g][s] if isinstance(parts[g][s], list) else [parts[g][s]])]
            for s in range(layers)
        ]

    lists = [every(codes), every(errors), every(inputs), every(grads)]
    own = (feats // tok, width // tok)
    if resident:
        dec_out, enc_out, bias_out = all_grads(*lists, sums, own, scale, layers)
        return enc_out, bias_out, dec_out
    me = lax.axis_index("tok")
    index = me.reshape(1).astype(jnp.int32)
    dec_out = dec_grads(*lists[:2], index, own[0], scale, layers)
    enc_out = enc_grads(*lists[2:], index, own[1], scale, layers)
    total = sum(sums[1:], sums[0]).reshape(layers, feats) * scale
    return enc_out, lax.dynamic_slice_in_dim(total, me * own[0], own[0], axis=1), dec_out


def solution(mesh):
    return jax.shard_map(
        shards,
        mesh=mesh,
        in_specs=(
            P(("tok", "feat"), None, None),
            P(("tok", "feat"), None, None),
            P(None, None, "feat"),
            P(None, "feat"),
            P(None, "feat", None),
        ),
        out_specs=(
            P(None, "tok", "feat"),
            P(None, ("feat", "tok")),
            P(None, ("feat", "tok"), None),
        ),
        check_vma=False,
    )
```

```python
import functools
import math

import jax
import jax.numpy as jnp
from jax import lax
from jax.experimental import pallas as pl
from jax.experimental.pallas import tpu as pltpu
from jax.sharding import PartitionSpec as P

MIB = 1 << 20


def pair_slot(source, target, layers):
    return sum((layers - k for k in range(source))) + (target - source)


def swap(value, axis, bits):
    return lax.ppermute(value, axis, [(i, i ^ bits) for i in range(lax.axis_size(axis))])


def cat(parts):
    return parts[0] if len(parts) == 1 else jnp.concatenate(parts, axis=0)


def dot(a, b, dims):
    return lax.dot_general(a, b, (dims, ((), ())), preferred_element_type=jnp.float32)


def piece(size, most):
    for c in range(most - most % 128, 0, -128):
        if size % c == 0:
            return c
    return size


def share(parts, own, me):
    if own % 128:
        return [(lax.dynamic_slice_in_dim(p, me[0] * own, own, axis=1), (p.shape[0], own), lambda j, me: (0, 0)) for p in parts]
    return [(p, (p.shape[0], own), lambda j, me: (0, me[0])) for p in parts]


def view(ref, block, index):
    at = []
    for size, most, i in zip(block, ref.shape, index):
        start = i * size
        at.append(slice(None) if size == most else pl.ds(start if isinstance(start, int) else pl.multiple_of(start, size), size))
    return ref.at[tuple(at)]


def inside(count):
    return [pl.BlockSpec(memory_space=pltpu.VMEM)] * count


def local(kernel, name, arrays, outs, after=(), flops=0):
    skip = len(after)
    return pl.pallas_call(
        lambda *refs: kernel(*refs[skip:]),
        name=name,
        out_shape=[pltpu.VMEM(s, d) for s, d in outs],
        in_specs=[pl.BlockSpec(memory_space=pl.ANY)] * skip
        + inside(len(arrays)),
        out_specs=inside(len(outs)),
        compiler_params=pltpu.CompilerParams(vmem_limit_bytes=4 * MIB),
        cost_estimate=pl.CostEstimate(flops=flops, bytes_accessed=0, transcendentals=0),
    )(*after, *[pltpu.with_memory_space_constraint(a, pltpu.VMEM) for a in arrays])


def steps_body(kernel, steps, ins, outs, *refs):
    for j in range(steps):
        kernel(*[view(r, b, m(j)) for r, (b, m) in zip(refs, ins + outs)])


def call(kernel, name, steps, ins, outs, flops, scalars=(), resident=False, after=()):
    if resident:
        body = functools.partial(steps_body, kernel, steps, [i[1:] for i in ins], [o[2:] for o in outs])
        return local(body, name, [i[0] for i in ins], [o[:2] for o in outs], after, flops)
    moved = sum(math.prod(a.shape) * a.dtype.itemsize for a, _, _ in ins)
    moved += sum(math.prod(s) * jnp.dtype(d).itemsize for s, d, _, _ in outs)
    return pl.pallas_call(
        kernel,
        name=name,
        out_shape=[jax.ShapeDtypeStruct(s, d) for s, d, _, _ in outs],
        grid_spec=pltpu.PrefetchScalarGridSpec(
            num_scalar_prefetch=len(scalars),
            grid=(steps,),
            in_specs=[pl.BlockSpec(b, m) for _, b, m in ins],
            out_specs=[pl.BlockSpec(b, m) for _, _, b, m in outs],
        ),
        compiler_params=pltpu.CompilerParams(vmem_limit_bytes=32 * MIB),
        cost_estimate=pl.CostEstimate(flops=flops, bytes_accessed=moved, transcendentals=0),
    )(*scalars, *[i[0] for i in ins])


def load_kernel(count, *refs):
    sources, places, sems = refs[:count], refs[count:2 * count], refs[2 * count]
    copies = [pltpu.make_async_copy(sources[i], places[i], sems.at[i]) for i in range(count)]
    for copy in copies:
        copy.start()
    for copy in copies:
        copy.wait()


def load(arrays, after=()):
    count, skip = len(arrays), len(after)
    return pl.pallas_call(
        lambda *refs: load_kernel(count, *refs[skip:]),
        name="load",
        out_shape=[pltpu.VMEM(a.shape, a.dtype) for a in arrays],
        in_specs=[pl.BlockSpec(memory_space=pl.ANY)] * skip + [pl.BlockSpec(memory_space=pltpu.HBM)] * count,
        out_specs=inside(count),
        scratch_shapes=[pltpu.SemaphoreType.DMA((count,))],
        compiler_params=pltpu.CompilerParams(vmem_limit_bytes=MIB),
        cost_estimate=pl.CostEstimate(flops=0, bytes_accessed=0, transcendentals=0),
    )(*after, *[pltpu.with_memory_space_constraint(a, pltpu.HBM) for a in arrays])


def wide(ref):
    return ref[...].astype(jnp.float32)


def join_kernel(groups, *refs):
    ins, outs = refs[:sum(len(g) for g in groups)], refs[sum(len(g) for g in groups):]
    for group, out in zip(groups, outs):
        values = [wide(r)[start:start + count] for r, (start, count) in zip(ins, group)]
        out[...] = cat(values).astype(out.dtype)
        ins = ins[len(group):]


def join(lists, after=()):
    lists = [[p if isinstance(p, tuple) else (p, 0, p.shape[0]) for p in parts] for parts in lists]
    outs = [((sum(c for _, _, c in parts), parts[0][0].shape[1]), parts[0][0].dtype) for parts in lists]
    kernel = functools.partial(join_kernel, [[p[1:] for p in parts] for parts in lists])
    return local(kernel, "join", [p[0] for parts in lists for p in parts], outs, after)


def pair_kernel(keep, *refs):
    got, (low, high) = refs[:-2], refs[-2:]
    part = wide(keep) + cat([wide(g) for g in got])
    half = part.shape[0] // 2
    low[...] = part[:half]
    high[...] = part[half:].astype(high.dtype)


def line_kernel(n, low, got, *outs):
    part = low[...] + wide(got)
    for k, out in enumerate(outs):
        out[...] = part[(k + 1) * n:(k + 2) * n].astype(out.dtype)


def open_kernel(n, count, low, got, *refs):
    line_kernel(n, low, got, *refs[-2 - count:-2])
    pair_kernel(*refs[:-2 - count], *refs[-2:])


def error_kernel(n, low, got, *refs):
    refs, target, out = refs[:-2], refs[-2], refs[-1]
    value = low[:n] + wide(got)[:n]
    for r in refs:
        value = value + wide(r)[:n]
    out[...] = (value - wide(target)).astype(out.dtype)


def turn_kernel(n, count, low, got, *refs):
    ends, (target, next_low, next_got), outs = refs[:count], refs[count:count + 3], refs[count + 3:]
    error_kernel(n, low, got, *ends, target, outs[-1])
    part = next_low[...] + wide(next_got)
    for k, out in enumerate(outs[:-1]):
        out[...] = cat([part[(k + 1) * n:(k + 2) * n], wide(outs[-1])]).astype(out.dtype)


def encode_kernel(parts, *refs):
    x = cat([r[...] for r in refs[:parts]])
    w, b, pre, code = refs[parts:]
    value = jnp.maximum(dot(x, w[0], ((1,), (0,))) + b[0], 0.0)
    pre[...] = value
    code[...] = (0.5 * value * value).astype(code.dtype)


def encode(source, parts, weight, bias, resident, after=()):
    _, width, feats = weight.shape
    m = sum(p.shape[0] for p in parts)
    c = piece(feats, 256)
    ins = [(p, p.shape, lambda j: (0, 0)) for p in parts]
    ins.append((weight, (1, width, c), lambda j: (source, 0, j)))
    ins.append((bias, (1, 1, c), lambda j: (source, 0, j)))
    outs = [((m, feats), d, (m, c), lambda j: (0, j)) for d in (jnp.float32, jnp.bfloat16)]
    return call(
        functools.partial(encode_kernel, len(parts)), "encode", feats // c, ins, outs, 2 * m * width * feats, (), resident, after
    )


def decode_kernel(sources, early, last, *refs):
    total = refs[2 * sources][...] if early else None
    for s in range(sources):
        term = dot(refs[s][...], refs[sources + s][0], ((1,), (0,)))
        total = term if total is None else total + term
    if not last:
        refs[-1][...] = total
        return
    keep, *gives = refs[2 * sources + early:]
    half = keep.shape[0]
    keep[...] = total[:half].astype(keep.dtype)
    size = half // len(gives)
    for k, give in enumerate(gives):
        give[...] = total[half + k * size:half + (k + 1) * size].astype(give.dtype)


def decode(target, sources, codes, weight, layers, early, last, resident, after=(), pieces=1):
    _, feats, width = weight.shape
    m = codes[0].shape[0]
    c = piece(width, 768)
    ins = [(codes[s], codes[s].shape, lambda j: (0, 0)) for s in sources]
    for s in sources:
        slot = pair_slot(s, target, layers)
        ins.append((weight, (1, feats, c), lambda j, slot=slot: (slot, 0, j)))
    ins += [(e, (m, c), lambda j: (0, j)) for e in early]
    outs = [((r, width), jnp.bfloat16, (r, c), lambda j: (0, j)) for r in [m // 2] + [m // 2 // pieces] * pieces]
    if not last:
        outs = [((m, width), jnp.float32, (m, c), lambda j: (0, j))]
    return call(
        functools.partial(decode_kernel, len(sources), len(early), last),
        "decode",
        width // c,
        ins,
        outs,
        2 * m * width * feats * len(sources),
        (),
        resident,
        after,
    )


def back_kernel(layers, counts, known, *refs):
    errors = []
    for count in counts:
        errors.append(cat([r[...] for r in refs[:count]]))
        refs = refs[count:]
    pre, refs = refs[:layers], refs[layers:]
    pairs = layers * (layers + 1) // 2
    weight, refs = refs[:pairs], refs[pairs:]
    early, refs = refs[:known], refs[known:]
    out, total = refs[:layers], refs[layers]
    for s in range(layers):
        value = early[s][...] if s < known else None
        for t in range(max(s, layers - 1 if s < known else 0), layers):
            term = dot(errors[t], weight[pair_slot(s, t, layers)][0], ((1,), (1,)))
            value = term if value is None else value + term
        value = (value * pre[s][...]).astype(out[s].dtype)
        out[s][...] = value
        total[s] = jnp.sum(value.astype(jnp.float32), axis=0, keepdims=True)


def back(errors, pre, weight, layers, resident, early=(), after=()):
    pairs, feats, width = weight.shape
    m = pre[0].shape[0]
    c = piece(feats, 256)
    ins = [(e, e.shape, lambda j: (0, 0)) for t in range(layers) for e in errors[t]]
    ins += [(p, (m, c), lambda j: (0, j)) for p in pre]
    ins += [(weight, (1, c, width), lambda j, k=k: (k, j, 0)) for k in range(pairs)]
    ins += [(e, (m, c), lambda j: (0, j)) for e in early]
    outs = [((m, feats), jnp.bfloat16, (m, c), lambda j: (0, j))] * layers
    outs.append(((layers, 1, feats), jnp.float32, (layers, 1, c), lambda j: (0, 0, j)))
    got = call(
        functools.partial(back_kernel, layers, [len(e) for e in errors], len(early)),
        "back",
        feats // c,
        ins,
        outs,
        2 * m * width * feats * (pairs - len(early)),
        (),
        resident,
        after,
    )
    return got[:layers], got[layers]


def first_kernel(parts, *refs):
    error = cat([r[...] for r in refs[:parts]])
    weight, out = refs[parts:]
    out[...] = dot(error, weight[0], ((1,), (1,)))


def first(errors, weight, after=()):
    _, feats, width = weight.shape
    m = sum(e.shape[0] for e in errors)
    c = piece(feats, 256)
    ins = [(e, e.shape, lambda j: (0, 0)) for e in errors]
    ins.append((weight, (1, c, width), lambda j: (0, j, 0)))
    outs = [((m, feats), jnp.float32, (m, c), lambda j: (0, j))]
    body = functools.partial(first_kernel, len(errors))
    return call(body, "first", feats // c, ins, outs, 2 * m * width * feats, (), True, after)[0]


def dec_kernel(layers, scale, counts, me, *refs):
    a, b = counts
    codes = [cat([r[...] for r in refs[s * a:(s + 1) * a]]) for s in range(layers)]
    refs = refs[layers * a:]
    errors = [cat([r[...] for r in refs[t * b:(t + 1) * b]]) for t in range(layers)]
    out = refs[layers * b]
    for s in range(layers):
        for t in range(s, layers):
            value = dot(codes[s], errors[t], ((0,), (0,))) * scale
            out[pair_slot(s, t, layers)] = value.astype(out.dtype)


def dec_grads(codes, errors, me, own, scale, layers):
    width = errors[0][0].shape[1]
    pairs = layers * (layers + 1) // 2
    m = sum(p.shape[0] for p in codes[0])
    c = piece(width, 768)
    ins = [i for s in range(layers) for i in share(codes[s], own, me)]
    ins += [(p, (p.shape[0], c), lambda j, me: (0, j)) for t in range(layers) for p in errors[t]]
    outs = [((pairs, own, width), jnp.bfloat16, (pairs, own, c), lambda j, me: (0, 0, j))]
    return call(
        functools.partial(dec_kernel, layers, scale, (len(codes[0]), len(errors[0]))),
        "dec_grads",
        width // c,
        ins,
        outs,
        2 * m * width * own * pairs,
        (me,),
    )[0]


def enc_kernel(layers, scale, counts, me, *refs):
    a, b = counts
    inputs = [cat([r[...] for r in refs[s * a:(s + 1) * a]]) for s in range(layers)]
    refs = refs[layers * a:]
    grads = [cat([r[...] for r in refs[s * b:(s + 1) * b]]) for s in range(layers)]
    out = refs[layers * b]
    for s in range(layers):
        out[s] = (dot(inputs[s], grads[s], ((0,), (0,))) * scale).astype(out.dtype)


def enc_grads(inputs, grads, me, own, scale, layers):
    feats = grads[0][0].shape[1]
    m = sum(p.shape[0] for p in inputs[0])
    c = piece(feats, 256)
    ins = [i for s in range(layers) for i in share(inputs[s], own, me)]
    ins += [(p, (p.shape[0], c), lambda j, me: (0, j)) for s in range(layers) for p in grads[s]]
    outs = [((layers, own, feats), jnp.bfloat16, (layers, own, c), lambda j, me: (0, 0, j))]
    return call(
        functools.partial(enc_kernel, layers, scale, (len(inputs[0]), len(grads[0]))),
        "enc_grads",
        feats // c,
        ins,
        outs,
        2 * m * own * feats * layers,
        (me,),
    )[0]


def grads_body(layers, scale, counts, own, *refs):
    lists = []
    for count in counts:
        lists.append([refs[s * count:(s + 1) * count] for s in range(layers)])
        refs = refs[layers * count:]
    codes, errors, inputs, grads = lists
    sums, refs = refs[:-7], refs[-7:]
    dec_out, enc_out, bias_out, dec_held, enc_held, dec_sems, enc_sems = refs
    copies = []
    me = lax.axis_index("tok")

    def mine(size):
        return pl.ds(pl.multiple_of(me * size, 128), size)

    def leave(held, out, sems, slot, left, right):
        width = right.shape[1]
        size = piece(width, 768)
        for j in range(width // size):
            value = dot(left, right[:, j * size:(j + 1) * size], ((0,), (0,)))
            at = (slot, slice(None), slice(j * size, (j + 1) * size))
            held[at] = (value * scale).astype(held.dtype)
            copy = pltpu.make_async_copy(held.at[at], out.at[at], sems.at[slot, j])
            copy.start()
            copies.append(copy)

    def columns(parts, size):
        if parts[0].shape[1] == size:
            return cat([p[...] for p in parts])
        return cat([p[:, mine(size)] for p in parts])

    for s in range(layers):
        left = columns(codes[s], own[0])
        for t in range(s, layers):
            right = cat([e[...] for e in errors[t]])
            leave(dec_held, dec_out, dec_sems, pair_slot(s, t, layers), left, right)
    for s in range(layers):
        leave(enc_held, enc_out, enc_sems, s, columns(inputs[s], own[1]), cat([g[...] for g in grads[s]]))
        total = sums[0][s, :, mine(own[0])]
        for more in sums[1:]:
            total = total + more[s, :, mine(own[0])]
        bias_out[pl.ds(s, 1)] = total * scale
    for copy in copies:
        copy.wait()


def all_grads(codes, errors, inputs, grads, sums, own, scale, layers):
    lists = (codes, errors, inputs, grads)
    dec = (layers * (layers + 1) // 2, own[0], errors[0][0].shape[1])
    enc = (layers, own[1], grads[0][0].shape[1])
    arrays = [pltpu.with_memory_space_constraint(p, pltpu.VMEM) for parts in lists for s in parts for p in s]
    arrays += [pltpu.with_memory_space_constraint(p, pltpu.VMEM) for p in sums]
    return pl.pallas_call(
        functools.partial(grads_body, layers, scale, [len(parts[0]) for parts in lists], own),
        name="grads",
        out_shape=[
            jax.ShapeDtypeStruct(dec, jnp.bfloat16),
            jax.ShapeDtypeStruct(enc, jnp.bfloat16),
            jax.ShapeDtypeStruct((layers, own[0]), jnp.float32),
        ],
        in_specs=inside(len(arrays)),
        out_specs=[pl.BlockSpec(memory_space=pltpu.HBM)] * 2 + inside(1),
        scratch_shapes=[
            pltpu.VMEM(dec, jnp.bfloat16),
            pltpu.VMEM(enc, jnp.bfloat16),
            pltpu.SemaphoreType.DMA((dec[0], dec[2] // piece(dec[2], 768))),
            pltpu.SemaphoreType.DMA((enc[0], enc[2] // piece(enc[2], 768))),
        ],
        compiler_params=pltpu.CompilerParams(vmem_limit_bytes=2 * (math.prod(dec) + math.prod(enc)) + 8 * MIB),
        cost_estimate=pl.CostEstimate(flops=0, bytes_accessed=0, transcendentals=0),
    )(*arrays)


def plain(acts_in, targets, enc_weight, bias, dec_weight, scale):
    layers, width, feats = enc_weight.shape
    feat, tok = lax.axis_size("feat"), lax.axis_size("tok")

    def gather(value):
        return lax.all_gather(value, "feat", axis=0, tiled=True)

    inputs, pre, codes, errors, grads, sums = [], [], [], [], [], []
    for g in range(tok):
        acts = swap(acts_in, "tok", g) if g else acts_in
        inputs.append([])
        pre.append([])
        codes.append([])
        for s in range(layers):
            inputs[g].append([gather(acts[:, s, :])])
            p, c = encode(s, inputs[g][s], enc_weight, bias, False)
            pre[g].append(p)
            codes[g].append(c)
    own = []
    for t in range(layers):
        halves = decode(t, range(t + 1), codes[0], dec_weight, layers, (), True, False)
        part = lax.psum_scatter(cat(halves), "feat", scatter_dimension=0, tiled=True)
        own.append((part.astype(jnp.float32) - targets[:, t, :].astype(jnp.float32)).astype(jnp.bfloat16))
    for g in range(tok):
        errors.append([[gather(swap(e, "tok", g) if g else e)] for e in own])
        d, total = back(errors[g], pre[g], dec_weight, layers, False)
        grads.append(d)
        sums.append(total)
    me = lax.axis_index("tok")
    index = me.reshape(1).astype(jnp.int32)

    def every(parts):
        return [[parts[g][s] for g in range(tok)] for s in range(layers)]

    def flat(parts):
        return [[parts[g][s][0] for g in range(tok)] for s in range(layers)]

    rows = feats // tok
    dec_out = dec_grads(every(codes), flat(errors), index, rows, scale, layers)
    enc_out = enc_grads(flat(inputs), every(grads), index, width // tok, scale, layers)
    total = sum(sums[1:], sums[0]).reshape(layers, feats) * scale
    return enc_out, lax.dynamic_slice_in_dim(total, me * rows, rows, axis=1), dec_out


def staged(acts_in, targets, enc_weight, bias, dec_weight, scale):
    layers, width, feats = enc_weight.shape
    n = acts_in.shape[0]
    quart = n * (lax.axis_size("feat") // 4)
    hop = quart // 2
    line = [4 * k for k in range(1, lax.axis_size("feat") // 4)]
    small = ((n, width), jnp.bfloat16)
    lows = [((quart, width), jnp.float32), ((quart, width), jnp.bfloat16)]

    def along(values):
        return [swap(v, "feat", bits) for v, bits in zip(values, line)]

    def across(value):
        return swap(value, "feat", 2)

    def core(value):
        return swap(value, "feat", 1)

    def away(value):
        return swap(value, "tok", 1)

    def encoded(s, parts, after=()):
        return encode(s, parts, enc_held, bias, True, after)

    def pair(keep, got, after):
        return local(pair_kernel, "pair", [keep, *got], lows, after)

    def error(t, low, got, ends, after):
        arrays = [low, got, *ends, targets[:, t, :]]
        return local(functools.partial(error_kernel, n), "error", arrays, [small], after)[0]

    acts = [acts_in[:, s, :] for s in range(layers)]
    ends = quart - n
    z_a0 = along([acts[0]] * len(line))
    enc_held = load([enc_weight])[0]
    done = [*z_a0, enc_held]
    line0, send, a1 = join([z_a0, [*z_a0, *acts], [acts[1]]], done)
    y_s, x_s = away(send), across(send)
    z_a1 = along([a1] * len(line))
    dec_held = load([dec_weight], [line0])[0]
    done = [*z_a1, x_s, y_s, dec_held]
    far0, far1 = [(x_s, ends, n), (x_s, 0, ends)], [(x_s, quart, n)]
    line1, col0 = join([z_a1, [acts[0], line0, *far0]], done)
    y_l1, x_l1 = away(line1), across(line1)
    in0 = [col0, core(col0)]
    pre0, code0 = encoded(0, in0)
    keep0, *give0 = decode(0, [0], [code0], dec_held, layers, (), True, True, (), 4)
    early = decode(1, [0], [code0], dec_held, layers, (), False, True, (keep0,))
    got0 = [core(g) for g in give0]
    done = [x_l1, y_l1, *got0, *early]
    low0, high0 = pair(keep0, got0, done)
    far1.append(x_l1)
    col1, fars = join([[a1, line1, *far1], far0 + far1], done)
    x_h0 = across(high0)
    in1 = [col1, core(col1)]
    pre1, code1 = encoded(1, in1)
    keep1, *give1 = decode(1, [1], [code0, code1], dec_held, layers, early, True, True, (), 4)
    got1 = [core(g) for g in give1]
    done = [x_h0, *got1]
    body = functools.partial(open_kernel, n, len(line))
    *ends0, low1, high1 = local(body, "open", [low0, x_h0, keep1, *got1], [small] * len(line) + lows, done)
    z_r0 = along(ends0)
    x_h1 = across(high1)
    done = [*z_r0, x_h1]
    arrays = [low0, x_h0, *z_r0, targets[:, 0, :], low1, x_h1]
    shapes = [((2 * n, width), jnp.bfloat16)] * len(line) + [small]
    *turned, e0 = local(functools.partial(turn_kernel, n, len(line)), "turn", arrays, shapes, done)
    y_f, y_e0, x_e0 = away(fars), away(e0), across(e0)
    z_t = along(turned)
    done = [*z_t, x_e0, y_e0, y_f]
    e1 = error(1, low1, x_h1, z_t, done)
    lines = [(z, n, n) for z in z_t]
    near0, both = join([[e0, *lines], [*lines, e1]], done)
    there0 = [(y_s, ends, n), (y_s, 0, ends), (y_f, 0, quart)]
    there0, there1 = join([there0, [(y_s, quart, n), y_l1, (y_f, quart, quart)]], done)
    y_b, x_b = away(both), across(both)
    z_e1 = along([e1] * len(line))
    there_in0, there_in1 = [there0, core(there0)], [there1, core(there1)]
    there_pre0, there_code0 = encoded(0, there_in0)
    there_pre1, there_code1 = encoded(1, there_in1)
    done = [*z_e1, x_b, y_b, there_code0, there_code1]
    near_y0 = [y_e0, (y_b, 0, ends)]
    half_y0 = [y_e0, (y_b, 0, hop - n)]
    near1, whole0, near_y0, go_x, go_y = join(
        [
            [e1, *z_e1],
            [near0, x_e0, (x_b, 0, ends)],
            near_y0,
            [*z_e1, *half_y0],
            [*z_e1, (x_b, hop - n, quart - hop)],
        ],
        done,
    )
    y_g, x_g = away(go_y), across(go_x)
    err0 = [whole0, core(whole0)]
    first_own = first(err0, dec_held)
    done = [x_g, y_g, first_own]
    whole1, one1, two1, near_y1, far_y0 = join(
        [
            [near1, (x_b, ends, n), (x_g, 0, ends)],
            [(y_b, ends, n), (y_g, 0, hop - n)],
            [(x_g, hop - n, quart - hop)],
            [(y_b, ends, n), (y_g, 0, ends)],
            [(x_g, ends, hop), (y_g, ends, quart - hop)],
        ],
        done,
    )
    y_t1, x_o1 = away(two1), across(one1)
    err1 = [whole1, core(whole1)]
    there_err0 = [near_y0, far_y0, core(near_y0), core(far_y0)]
    core_n1 = core(near_y1)
    grad_own, sum_own = back([err0, err1], [pre0, pre1], dec_held, layers, True, [first_own])
    first_there = first(there_err0, dec_held, [grad_own[0]])
    done = [x_o1, y_t1, core_n1, first_there]
    far_y1 = join([[x_o1, y_t1]], done)[0]
    there_err1 = [near_y1, far_y1, core_n1, core(far_y1)]
    there_errs, there_pres = [there_err0, there_err1], [there_pre0, there_pre1]
    grad_there, sum_there = back(there_errs, there_pres, dec_held, layers, True, [first_there])
    dec_out, enc_out, bias_out = all_grads(
        [[code0, there_code0], [code1, there_code1]],
        [err0 + there_err0, err1 + there_err1],
        [in0 + there_in0, in1 + there_in1],
        [[grad_own[s], grad_there[s]] for s in range(layers)],
        [sum_own, sum_there],
        (feats // lax.axis_size("tok"), width // lax.axis_size("tok")),
        scale,
        layers,
    )
    return enc_out, bias_out, dec_out


def shards(acts_in, targets, enc_weight, enc_bias, dec_weight):
    layers, width, feats = enc_weight.shape
    n = acts_in.shape[0]
    feat, tok = lax.axis_size("feat"), lax.axis_size("tok")
    scale = 1.0 / math.sqrt(n * feat * tok)
    bias = enc_bias.reshape(layers, 1, feats)
    held = 2 * (math.prod(enc_weight.shape) + math.prod(dec_weight.shape))
    held += 4 * layers * n * feat * tok * (width + 2 * feats)
    fits = held <= 54 * MIB and n % 8 == 0 and (feats // tok) % 128 == 0 and (width // tok) % 128 == 0
    run = staged if fits and layers == 2 and tok == 2 and feat >= 8 else plain
    return run(acts_in, targets, enc_weight, bias, dec_weight, scale)


def solution(mesh):
    return jax.shard_map(
        shards,
        mesh=mesh,
        in_specs=(
            P(("tok", "feat"), None, None),
            P(("tok", "feat"), None, None),
            P(None, None, "feat"),
            P(None, "feat"),
            P(None, "feat", None),
        ),
        out_specs=(
            P(None, "tok", "feat"),
            P(None, ("feat", "tok")),
            P(None, ("feat", "tok"), None),
        ),
        check_vma=False,
    )
```

```python
import functools
import math

import jax
import jax.numpy as jnp
from jax import lax
from jax.experimental import pallas as pl
from jax.experimental.pallas import tpu as pltpu
from jax.sharding import PartitionSpec as P

MIB = 1 << 20


def pair_slot(source, target, layers):
    return sum((layers - k for k in range(source))) + (target - source)


def swap(value, axis, bits):
    return lax.ppermute(value, axis, [(i, i ^ bits) for i in range(lax.axis_size(axis))])


def cat(parts):
    return parts[0] if len(parts) == 1 else jnp.concatenate(parts, axis=0)


def dot(a, b, dims):
    return lax.dot_general(a, b, (dims, ((), ())), preferred_element_type=jnp.float32)


def piece(size, most):
    for c in range(most - most % 128, 0, -128):
        if size % c == 0:
            return c
    return size


def share(parts, own, me):
    if own % 128:
        return [(lax.dynamic_slice_in_dim(p, me[0] * own, own, axis=1), (p.shape[0], own), lambda j, me: (0, 0)) for p in parts]
    return [(p, (p.shape[0], own), lambda j, me: (0, me[0])) for p in parts]


def view(ref, block, index):
    at = []
    for size, most, i in zip(block, ref.shape, index):
        start = i * size
        at.append(slice(None) if size == most else pl.ds(start if isinstance(start, int) else pl.multiple_of(start, size), size))
    return ref.at[tuple(at)]


def inside(count):
    return [pl.BlockSpec(memory_space=pltpu.VMEM)] * count


def local(kernel, name, arrays, outs, after=(), flops=0):
    skip = len(after)
    return pl.pallas_call(
        lambda *refs: kernel(*refs[skip:]),
        name=name,
        out_shape=[pltpu.VMEM(s, d) for s, d in outs],
        in_specs=[pl.BlockSpec(memory_space=pl.ANY)] * skip
        + inside(len(arrays)),
        out_specs=inside(len(outs)),
        compiler_params=pltpu.CompilerParams(vmem_limit_bytes=4 * MIB),
        cost_estimate=pl.CostEstimate(flops=flops, bytes_accessed=0, transcendentals=0),
    )(*after, *[pltpu.with_memory_space_constraint(a, pltpu.VMEM) for a in arrays])


def steps_body(kernel, steps, ins, outs, *refs):
    for j in range(steps):
        kernel(*[view(r, b, m(j)) for r, (b, m) in zip(refs, ins + outs)])


def call(kernel, name, steps, ins, outs, flops, scalars=(), resident=False, after=()):
    if resident:
        body = functools.partial(steps_body, kernel, steps, [i[1:] for i in ins], [o[2:] for o in outs])
        return local(body, name, [i[0] for i in ins], [o[:2] for o in outs], after, flops)
    moved = sum(math.prod(a.shape) * a.dtype.itemsize for a, _, _ in ins)
    moved += sum(math.prod(s) * jnp.dtype(d).itemsize for s, d, _, _ in outs)
    return pl.pallas_call(
        kernel,
        name=name,
        out_shape=[jax.ShapeDtypeStruct(s, d) for s, d, _, _ in outs],
        grid_spec=pltpu.PrefetchScalarGridSpec(
            num_scalar_prefetch=len(scalars),
            grid=(steps,),
            in_specs=[pl.BlockSpec(b, m) for _, b, m in ins],
            out_specs=[pl.BlockSpec(b, m) for _, _, b, m in outs],
        ),
        compiler_params=pltpu.CompilerParams(vmem_limit_bytes=32 * MIB),
        cost_estimate=pl.CostEstimate(flops=flops, bytes_accessed=moved, transcendentals=0),
    )(*scalars, *[i[0] for i in ins])


def load_kernel(count, *refs):
    sources, places, sems = refs[:count], refs[count:2 * count], refs[2 * count]
    copies = [pltpu.make_async_copy(sources[i], places[i], sems.at[i]) for i in range(count)]
    for copy in copies:
        copy.start()
    for copy in copies:
        copy.wait()


def load(arrays, after=()):
    count, skip = len(arrays), len(after)
    return pl.pallas_call(
        lambda *refs: load_kernel(count, *refs[skip:]),
        name="load",
        out_shape=[pltpu.VMEM(a.shape, a.dtype) for a in arrays],
        in_specs=[pl.BlockSpec(memory_space=pl.ANY)] * skip + [pl.BlockSpec(memory_space=pltpu.HBM)] * count,
        out_specs=inside(count),
        scratch_shapes=[pltpu.SemaphoreType.DMA((count,))],
        compiler_params=pltpu.CompilerParams(vmem_limit_bytes=MIB),
        cost_estimate=pl.CostEstimate(flops=0, bytes_accessed=0, transcendentals=0),
    )(*after, *[pltpu.with_memory_space_constraint(a, pltpu.HBM) for a in arrays])


def wide(ref):
    return ref[...].astype(jnp.float32)


def join_kernel(groups, *refs):
    ins, outs = refs[:sum(len(g) for g in groups)], refs[sum(len(g) for g in groups):]
    for group, out in zip(groups, outs):
        values = [wide(r)[start:start + count] for r, (start, count) in zip(ins, group)]
        out[...] = cat(values).astype(out.dtype)
        ins = ins[len(group):]


def join(lists, after=(), flops=0):
    lists = [[p if isinstance(p, tuple) else (p, 0, p.shape[0]) for p in parts] for parts in lists]
    outs = [((sum(c for _, _, c in parts), parts[0][0].shape[1]), parts[0][0].dtype) for parts in lists]
    kernel = functools.partial(join_kernel, [[p[1:] for p in parts] for parts in lists])
    return local(kernel, "join", [p[0] for parts in lists for p in parts], outs, after, flops)


def pair_kernel(keep, *refs):
    got, (low, high) = refs[:-2], refs[-2:]
    part = wide(keep) + cat([wide(g) for g in got])
    half = part.shape[0] // 2
    low[...] = part[:half]
    high[...] = part[half:].astype(high.dtype)


def line_kernel(n, low, got, *outs):
    part = low[...] + wide(got)
    for k, out in enumerate(outs):
        out[...] = part[(k + 1) * n:(k + 2) * n].astype(out.dtype)


def open_kernel(n, count, low, got, *refs):
    line_kernel(n, low, got, *refs[-2 - count:-2])
    pair_kernel(*refs[:-2 - count], *refs[-2:])


def error_kernel(n, low, got, *refs):
    refs, target, out = refs[:-2], refs[-2], refs[-1]
    value = low[:n] + wide(got)[:n]
    for r in refs:
        value = value + wide(r)[:n]
    out[...] = (value - wide(target)).astype(out.dtype)


def turn_kernel(n, count, low, got, *refs):
    ends, (target, next_low, next_got), outs = refs[:count], refs[count:count + 3], refs[count + 3:]
    error_kernel(n, low, got, *ends, target, outs[-1])
    part = next_low[...] + wide(next_got)
    for k, out in enumerate(outs[:-1]):
        out[...] = cat([part[(k + 1) * n:(k + 2) * n], wide(outs[-1])]).astype(out.dtype)


def encode_kernel(parts, *refs):
    x = cat([r[...] for r in refs[:parts]])
    w, b, pre, code = refs[parts:]
    value = jnp.maximum(dot(x, w[0], ((1,), (0,))) + b[0], 0.0)
    pre[...] = value
    code[...] = (0.5 * value * value).astype(code.dtype)


def encode(source, parts, weight, bias, resident, after=()):
    _, width, feats = weight.shape
    m = sum(p.shape[0] for p in parts)
    c = piece(feats, 256)
    ins = [(p, p.shape, lambda j: (0, 0)) for p in parts]
    ins.append((weight, (1, width, c), lambda j: (source, 0, j)))
    ins.append((bias, (1, 1, c), lambda j: (source, 0, j)))
    outs = [((m, feats), d, (m, c), lambda j: (0, j)) for d in (jnp.float32, jnp.bfloat16)]
    return call(
        functools.partial(encode_kernel, len(parts)), "encode", feats // c, ins, outs, 2 * m * width * feats, (), resident, after
    )


def decode_kernel(sources, early, last, *refs):
    total = refs[2 * sources][...] if early else None
    for s in range(sources):
        term = dot(refs[s][...], refs[sources + s][0], ((1,), (0,)))
        total = term if total is None else total + term
    if not last:
        refs[-1][...] = total
        return
    keep, *gives = refs[2 * sources + early:]
    half = keep.shape[0]
    keep[...] = total[:half].astype(keep.dtype)
    size = half // len(gives)
    for k, give in enumerate(gives):
        give[...] = total[half + k * size:half + (k + 1) * size].astype(give.dtype)


def decode(target, sources, codes, weight, layers, early, last, resident, after=(), pieces=1):
    _, feats, width = weight.shape
    m = codes[0].shape[0]
    c = piece(width, 768)
    ins = [(codes[s], codes[s].shape, lambda j: (0, 0)) for s in sources]
    for s in sources:
        slot = pair_slot(s, target, layers)
        ins.append((weight, (1, feats, c), lambda j, slot=slot: (slot, 0, j)))
    ins += [(e, (m, c), lambda j: (0, j)) for e in early]
    outs = [((r, width), jnp.bfloat16, (r, c), lambda j: (0, j)) for r in [m // 2] + [m // 2 // pieces] * pieces]
    if not last:
        outs = [((m, width), jnp.float32, (m, c), lambda j: (0, j))]
    return call(
        functools.partial(decode_kernel, len(sources), len(early), last),
        "decode",
        width // c,
        ins,
        outs,
        2 * m * width * feats * len(sources),
        (),
        resident,
        after,
    )


def some(part):
    return part if isinstance(part, tuple) else (part, 0, part.shape[0])


def back_kernel(layers, counts, parts, known, *refs):
    errors = []
    for count in counts:
        errors.append(cat([r[...] for r in refs[:count]]))
        refs = refs[count:]
    pre = []
    for _ in range(layers):
        pre.append(cat([r[...] for r in refs[:parts]]))
        refs = refs[parts:]
    pairs = layers * (layers + 1) // 2
    weight, refs = refs[:pairs], refs[pairs:]
    early, refs = refs[:known], refs[known:]
    out, total = refs[:layers], refs[layers]
    for s in range(layers):
        value = early[s][...] if s < known else None
        for t in range(max(s, layers - 1 if s < known else 0), layers):
            term = dot(errors[t], weight[pair_slot(s, t, layers)][0], ((1,), (1,)))
            value = term if value is None else value + term
        value = (value * pre[s]).astype(out[s].dtype)
        out[s][...] = value
        total[s] = jnp.sum(value.astype(jnp.float32), axis=0, keepdims=True)


def back(errors, pre, weight, layers, resident, early=(), after=()):
    pairs, feats, width = weight.shape
    errors, pre = ([[some(p) for p in parts] for parts in lists] for lists in (errors, pre))
    m = sum(count for _, _, count in pre[0])
    c = piece(feats, 256)
    ins = [(e, (r, width), lambda j, i=i // r: (i, 0)) for parts in errors for e, i, r in parts]
    ins += [(p, (r, c), lambda j, i=i // r: (i, j)) for parts in pre for p, i, r in parts]
    ins += [(weight, (1, c, width), lambda j, k=k: (k, j, 0)) for k in range(pairs)]
    ins += [(e, (m, c), lambda j: (0, j)) for e in early]
    outs = [((m, feats), jnp.bfloat16, (m, c), lambda j: (0, j))] * layers
    outs.append(((layers, 1, feats), jnp.float32, (layers, 1, c), lambda j: (0, 0, j)))
    got = call(
        functools.partial(back_kernel, layers, [len(e) for e in errors], len(pre[0]), len(early)),
        "back",
        feats // c,
        ins,
        outs,
        2 * m * width * feats * (pairs - len(early)),
        (),
        resident,
        after,
    )
    return got[:layers], got[layers]


def first_kernel(parts, *refs):
    error = cat([r[...] for r in refs[:parts]])
    weight, out = refs[parts:]
    out[...] = dot(error, weight[0], ((1,), (1,)))


def first(errors, weight, after=()):
    _, feats, width = weight.shape
    m = sum(e.shape[0] for e in errors)
    c = piece(feats, 256)
    ins = [(e, e.shape, lambda j: (0, 0)) for e in errors]
    ins.append((weight, (1, c, width), lambda j: (0, j, 0)))
    outs = [((m, feats), jnp.float32, (m, c), lambda j: (0, j))]
    body = functools.partial(first_kernel, len(errors))
    return call(body, "first", feats // c, ins, outs, 2 * m * width * feats, (), True, after)[0]


def dec_kernel(layers, scale, counts, me, *refs):
    a, b = counts
    codes = [cat([r[...] for r in refs[s * a:(s + 1) * a]]) for s in range(layers)]
    refs = refs[layers * a:]
    errors = [cat([r[...] for r in refs[t * b:(t + 1) * b]]) for t in range(layers)]
    out = refs[layers * b]
    for s in range(layers):
        for t in range(s, layers):
            value = dot(codes[s], errors[t], ((0,), (0,))) * scale
            out[pair_slot(s, t, layers)] = value.astype(out.dtype)


def dec_grads(codes, errors, me, own, scale, layers):
    width = errors[0][0].shape[1]
    pairs = layers * (layers + 1) // 2
    m = sum(p.shape[0] for p in codes[0])
    c = piece(width, 768)
    ins = [i for s in range(layers) for i in share(codes[s], own, me)]
    ins += [(p, (p.shape[0], c), lambda j, me: (0, j)) for t in range(layers) for p in errors[t]]
    outs = [((pairs, own, width), jnp.bfloat16, (pairs, own, c), lambda j, me: (0, 0, j))]
    return call(
        functools.partial(dec_kernel, layers, scale, (len(codes[0]), len(errors[0]))),
        "dec_grads",
        width // c,
        ins,
        outs,
        2 * m * width * own * pairs,
        (me,),
    )[0]


def enc_kernel(layers, scale, counts, me, *refs):
    a, b = counts
    inputs = [cat([r[...] for r in refs[s * a:(s + 1) * a]]) for s in range(layers)]
    refs = refs[layers * a:]
    grads = [cat([r[...] for r in refs[s * b:(s + 1) * b]]) for s in range(layers)]
    out = refs[layers * b]
    for s in range(layers):
        out[s] = (dot(inputs[s], grads[s], ((0,), (0,))) * scale).astype(out.dtype)


def enc_grads(inputs, grads, me, own, scale, layers):
    feats = grads[0][0].shape[1]
    m = sum(p.shape[0] for p in inputs[0])
    c = piece(feats, 256)
    ins = [i for s in range(layers) for i in share(inputs[s], own, me)]
    ins += [(p, (p.shape[0], c), lambda j, me: (0, j)) for s in range(layers) for p in grads[s]]
    outs = [((layers, own, feats), jnp.bfloat16, (layers, own, c), lambda j, me: (0, 0, j))]
    return call(
        functools.partial(enc_kernel, layers, scale, (len(inputs[0]), len(grads[0]))),
        "enc_grads",
        feats // c,
        ins,
        outs,
        2 * m * own * feats * layers,
        (me,),
    )[0]


def mine(size):
    return pl.ds(pl.multiple_of(lax.axis_index("tok") * size, 128), size)


def gathered(parts, size):
    at = slice(None) if parts[0][0].shape[1] == size else mine(size)
    return cat([p[start:start + count, at] for p, (start, count) in parts])


def ahead_kernel(rows, own, *refs):
    *ins, out = refs
    count = len(rows[0])
    left = gathered(list(zip(ins[:count], rows[0])), own)
    right = gathered(list(zip(ins[count:], rows[1])), out.shape[1])
    size = piece(right.shape[1], 768)
    for j in range(right.shape[1] // size):
        at = slice(j * size, (j + 1) * size)
        out[:, at] = dot(left, right[:, at], ((0,), (0,)))


def ahead(codes, errors, own):
    lists = [[some(p) for p in parts] for parts in (codes, errors)]
    rows = [[p[1:] for p in parts] for parts in lists]
    arrays = [p[0] for parts in lists for p in parts]
    out = ((own, arrays[-1].shape[1]), jnp.float32)
    flops = 2 * math.prod(out[0]) * sum(r[1] for r in rows[0])
    return local(functools.partial(ahead_kernel, rows, own), "ahead", arrays, [out], (), flops)[0]


def grads_body(layers, scale, rows, own, late, *refs):
    lists = []
    for parts in rows:
        lists.append([])
        for bounds in parts:
            lists[-1].append(list(zip(refs, bounds)))
            refs = refs[len(bounds):]
    codes, errors, inputs, grads = lists
    early, sums, refs = refs[0], refs[1:-7], refs[-7:]
    dec_out, enc_out, bias_out, dec_held, enc_held, dec_sems, enc_sems = refs
    copies = []
    def leave(held, out, sems, slot, left, right, before=None):
        width = right.shape[1]
        size = piece(width, 768)
        for j in range(width // size):
            value = dot(left, right[:, j * size:(j + 1) * size], ((0,), (0,)))
            if before is not None:
                value = value + before[:, j * size:(j + 1) * size]
            at = (slot, slice(None), slice(j * size, (j + 1) * size))
            held[at] = (value * scale).astype(held.dtype)
            copy = pltpu.make_async_copy(held.at[at], out.at[at], sems.at[slot, j])
            copy.start()
            copies.append(copy)

    for s in range(layers):
        left = gathered(codes[s], own[0])
        for t in range(s, layers):
            slot, before, first = pair_slot(s, t, layers), None, left
            right = errors[t]
            if slot == 0:
                before, first, right = early, gathered(codes[s][-late:], own[0]), right[-late:]
            leave(dec_held, dec_out, dec_sems, slot, first, gathered(right, dec_out.shape[2]), before)
    for s in range(layers):
        leave(enc_held, enc_out, enc_sems, s, gathered(inputs[s], own[1]), gathered(grads[s], enc_out.shape[2]))
        total = sums[0][s, :, mine(own[0])]
        for more in sums[1:]:
            total = total + more[s, :, mine(own[0])]
        bias_out[pl.ds(s, 1)] = total * scale
    for copy in copies:
        copy.wait()


def all_grads(codes, errors, inputs, grads, early, late, sums, own, scale, layers):
    lists = [[[some(p) for p in parts] for parts in each] for each in (codes, errors, inputs, grads)]
    rows = [[[p[1:] for p in parts] for parts in each] for each in lists]
    dec = (layers * (layers + 1) // 2, own[0], lists[1][0][0][0].shape[1])
    enc = (layers, own[1], lists[3][0][0][0].shape[1])
    arrays = [p[0] for each in lists for parts in each for p in parts] + [early, *sums]
    arrays = [pltpu.with_memory_space_constraint(a, pltpu.VMEM) for a in arrays]
    return pl.pallas_call(
        functools.partial(grads_body, layers, scale, rows, own, late),
        name="grads",
        out_shape=[
            jax.ShapeDtypeStruct(dec, jnp.bfloat16),
            jax.ShapeDtypeStruct(enc, jnp.bfloat16),
            jax.ShapeDtypeStruct((layers, own[0]), jnp.float32),
        ],
        in_specs=inside(len(arrays)),
        out_specs=[pl.BlockSpec(memory_space=pltpu.HBM)] * 2 + inside(1),
        scratch_shapes=[
            pltpu.VMEM(dec, jnp.bfloat16),
            pltpu.VMEM(enc, jnp.bfloat16),
            pltpu.SemaphoreType.DMA((dec[0], dec[2] // piece(dec[2], 768))),
            pltpu.SemaphoreType.DMA((enc[0], enc[2] // piece(enc[2], 768))),
        ],
        compiler_params=pltpu.CompilerParams(vmem_limit_bytes=2 * (math.prod(dec) + math.prod(enc)) + 8 * MIB),
        cost_estimate=pl.CostEstimate(flops=0, bytes_accessed=0, transcendentals=0),
    )(*arrays)


def plain(acts_in, targets, enc_weight, bias, dec_weight, scale):
    layers, width, feats = enc_weight.shape
    feat, tok = lax.axis_size("feat"), lax.axis_size("tok")

    def gather(value):
        return lax.all_gather(value, "feat", axis=0, tiled=True)

    inputs, pre, codes, errors, grads, sums = [], [], [], [], [], []
    for g in range(tok):
        acts = swap(acts_in, "tok", g) if g else acts_in
        inputs.append([])
        pre.append([])
        codes.append([])
        for s in range(layers):
            inputs[g].append([gather(acts[:, s, :])])
            p, c = encode(s, inputs[g][s], enc_weight, bias, False)
            pre[g].append(p)
            codes[g].append(c)
    own = []
    for t in range(layers):
        halves = decode(t, range(t + 1), codes[0], dec_weight, layers, (), True, False)
        part = lax.psum_scatter(cat(halves), "feat", scatter_dimension=0, tiled=True)
        own.append((part.astype(jnp.float32) - targets[:, t, :].astype(jnp.float32)).astype(jnp.bfloat16))
    for g in range(tok):
        errors.append([[gather(swap(e, "tok", g) if g else e)] for e in own])
        d, total = back(errors[g], [[p] for p in pre[g]], dec_weight, layers, False)
        grads.append(d)
        sums.append(total)
    me = lax.axis_index("tok")
    index = me.reshape(1).astype(jnp.int32)

    def every(parts):
        return [[parts[g][s] for g in range(tok)] for s in range(layers)]

    def flat(parts):
        return [[parts[g][s][0] for g in range(tok)] for s in range(layers)]

    rows = feats // tok
    dec_out = dec_grads(every(codes), flat(errors), index, rows, scale, layers)
    enc_out = enc_grads(flat(inputs), every(grads), index, width // tok, scale, layers)
    total = sum(sums[1:], sums[0]).reshape(layers, feats) * scale
    return enc_out, lax.dynamic_slice_in_dim(total, me * rows, rows, axis=1), dec_out


def staged(acts_in, targets, enc_weight, bias, dec_weight, scale):
    layers, width, feats = enc_weight.shape
    n = acts_in.shape[0]
    quart = n * (lax.axis_size("feat") // 4)
    hop = quart // 2
    line = [4 * k for k in range(1, lax.axis_size("feat") // 4)]
    small = ((n, width), jnp.bfloat16)
    lows = [((quart, width), jnp.float32), ((quart, width), jnp.bfloat16)]

    def along(values):
        return [swap(v, "feat", bits) for v, bits in zip(values, line)]

    def across(value):
        return swap(value, "feat", 2)

    def core(value):
        return swap(value, "feat", 1)

    def away(value):
        return swap(value, "tok", 1)

    def encoded(s, parts, after=()):
        return encode(s, parts, enc_held, bias, True, after)

    def pair(keep, got, after):
        return local(pair_kernel, "pair", [keep, *got], lows, after)

    def error(t, low, got, ends, after):
        arrays = [low, got, *ends, targets[:, t, :]]
        return local(functools.partial(error_kernel, n), "error", arrays, [small], after)[0]

    def nears(parts):
        return [(p, 0, quart) for p in parts]

    def fars(parts):
        return [(p, quart, quart) for p in parts]

    def halves(value):
        return [(value, k * quart, quart) for k in (0, 2)], [(value, k * quart, quart) for k in (1, 3)]

    acts = [acts_in[:, s, :] for s in range(layers)]
    ends = quart - n
    z_a0 = along([acts[0]] * len(line))
    enc_held = load([enc_weight])[0]
    done = [*z_a0, enc_held]
    line0, send, a1 = join([z_a0, [*z_a0, *acts], [acts[1]]], done)
    y_s, x_s = away(send), across(send)
    z_a1 = along([a1] * len(line))
    dec_held = load([dec_weight], [line0])[0]
    done = [*z_a1, x_s, y_s, dec_held]
    far0, far1 = [(x_s, ends, n), (x_s, 0, ends)], [(x_s, quart, n)]
    line1, col0 = join([z_a1, [acts[0], line0, *far0]], done)
    x_l1 = across(line1)
    in0 = [col0, core(col0)]
    pre0, code0 = encoded(0, in0)
    keep0, *give0 = decode(0, [0], [code0], dec_held, layers, (), True, True, (), 3)
    got0 = [core(g) for g in give0]
    done = [x_l1, *got0]
    low0, high0 = pair(keep0, got0, done)
    far1.append(x_l1)
    col1, far_both = join([[a1, line1, *far1], far0 + far1], done)
    y_l1, x_h0 = away(line1), across(high0)
    in1 = [col1, core(col1)]
    early = decode(1, [0], [code0], dec_held, layers, (), False, True, (low0, col1))
    pre1, code1 = encoded(1, in1, early)
    keep1, *give1 = decode(1, [1], [code0, code1], dec_held, layers, early, True, True, (), 3)
    got1 = [core(g) for g in give1]
    done = [x_h0, y_l1, *got1]
    body = functools.partial(open_kernel, n, len(line))
    *ends0, low1, high1 = local(body, "open", [low0, x_h0, keep1, *got1], [small] * len(line) + lows, done)
    z_r0 = along(ends0)
    x_h1 = across(high1)
    done = [*z_r0, x_h1]
    target = join([[targets[:, 0, :]]], [low1], 2 * quart * width * feats)[0]
    arrays = [low0, x_h0, *z_r0, target, low1, x_h1]
    shapes = [((2 * n, width), jnp.bfloat16)] * len(line) + [small]
    *turned, e0 = local(functools.partial(turn_kernel, n, len(line)), "turn", arrays, shapes, done)
    y_f, y_e0, x_e0 = away(far_both), away(e0), across(e0)
    z_t = along(turned)
    done = [*z_t, x_e0, y_e0, y_f]
    e1 = error(1, low1, x_h1, z_t, done)
    lines = [(z, n, n) for z in z_t]
    near0, both = join([[e0, *lines], [*lines, e1]], done)
    there0 = [(y_s, ends, n), (y_s, 0, ends), (y_f, 0, quart)]
    there0, there1 = join([there0, [(y_s, quart, n), y_l1, (y_f, quart, quart)]], done)
    y_b, x_b = away(both), across(both)
    z_e1 = along([e1] * len(line))
    there_in0, there_in1 = [there0, core(there0)], [there1, core(there1)]
    there_pre0, there_code0 = encoded(0, there_in0)
    there_pre1, there_code1 = encoded(1, there_in1)
    done = [*z_e1, x_b, y_b, there_code0, there_code1]
    near1, whole0, near_y0, send = join(
        [[e1, *z_e1], [near0, x_e0, (x_b, 0, ends)], [y_e0, (y_b, 0, ends)], z_e1], done
    )
    y_g, x_g = away(send), across(send)
    err0 = [whole0, core(whole0)]
    near_err0 = [near_y0, core(near_y0)]
    first_own = first(err0, dec_held)
    first_near = first(near_err0, dec_held)
    share = (feats // lax.axis_size("tok"), width // lax.axis_size("tok"))
    early = ahead([code0] + halves(there_code0)[0], err0 + near_err0, share[0])
    done = [x_g, y_g, first_own, first_near, early]
    whole1, near_y1, go_x, go_y = join(
        [
            [near1, (x_b, ends, n), x_g],
            [(y_b, ends, n), y_g],
            [(near_y0, 0, hop), (y_b, ends, n), (y_g, 0, hop - n)],
            [(x_b, hop - n, quart - hop), (x_g, hop - n, quart - hop)],
        ],
        done,
    )
    y_t, x_o = away(go_y), across(go_x)
    err1 = [whole1, core(whole1)]
    near_err1 = [near_y1, core(near_y1)]

    near_pre, far_pre = zip(halves(there_pre0), halves(there_pre1))
    grad_own, sum_own = back([err0, err1], [[pre0], [pre1]], dec_held, layers, True, [first_own])
    grad_near, sum_near = back([near_err0, near_err1], near_pre, dec_held, layers, True, [first_near])
    done = [x_o, y_t, grad_own[0], grad_near[0]]
    left = quart - hop
    far = join([[(x_o, 0, hop), (y_t, 0, left), (x_o, hop, hop), (y_t, left, left)]], done)[0]
    far = [far, core(far)]
    far_errs = [nears(far), fars(far)]
    grad_far, sum_far = back(far_errs, far_pre, dec_held, layers, True)
    codes = [sum(halves(c), []) for c in (there_code0, there_code1)]
    seen = [nears(p) + fars(p) for p in (there_in0, there_in1)]
    dec_out, enc_out, bias_out = all_grads(
        [[code0] + codes[0], [code1] + codes[1]],
        [err0 + near_err0 + far_errs[0], err1 + near_err1 + far_errs[1]],
        [in0 + seen[0], in1 + seen[1]],
        [[grad_own[s], grad_near[s], grad_far[s]] for s in range(layers)],
        early,
        2,
        [sum_own, sum_near, sum_far],
        share,
        scale,
        layers,
    )
    return enc_out, bias_out, dec_out


def shards(acts_in, targets, enc_weight, enc_bias, dec_weight):
    layers, width, feats = enc_weight.shape
    n = acts_in.shape[0]
    feat, tok = lax.axis_size("feat"), lax.axis_size("tok")
    scale = 1.0 / math.sqrt(n * feat * tok)
    bias = enc_bias.reshape(layers, 1, feats)
    held = 2 * (math.prod(enc_weight.shape) + math.prod(dec_weight.shape))
    held += 4 * layers * n * feat * tok * (width + 2 * feats)
    fits = held <= 54 * MIB and n % 8 == 0 and (feats // tok) % 128 == 0 and (width // tok) % 128 == 0
    run = staged if fits and layers == 2 and tok == 2 and feat >= 8 else plain
    return run(acts_in, targets, enc_weight, bias, dec_weight, scale)


def solution(mesh):
    return jax.shard_map(
        shards,
        mesh=mesh,
        in_specs=(
            P(("tok", "feat"), None, None),
            P(("tok", "feat"), None, None),
            P(None, None, "feat"),
            P(None, "feat"),
            P(None, "feat", None),
        ),
        out_specs=(
            P(None, "tok", "feat"),
            P(None, ("feat", "tok")),
            P(None, ("feat", "tok"), None),
        ),
        check_vma=False,
    )
```

```python
import functools
import math

import jax
import jax.numpy as jnp
from jax import lax
from jax.experimental import pallas as pl
from jax.experimental.pallas import tpu as pltpu
from jax.sharding import PartitionSpec as P

MIB = 1 << 20


def pair_slot(source, target, layers):
    return sum((layers - k for k in range(source))) + (target - source)


def swap(value, axis, bits):
    return lax.ppermute(value, axis, [(i, i ^ bits) for i in range(lax.axis_size(axis))])


def cat(parts):
    return parts[0] if len(parts) == 1 else jnp.concatenate(parts, axis=0)


def dot(a, b, dims):
    return lax.dot_general(a, b, (dims, ((), ())), preferred_element_type=jnp.float32)


def piece(size, most):
    for c in range(most - most % 128, 0, -128):
        if size % c == 0:
            return c
    return size


def share(parts, own, me):
    if own % 128:
        return [(lax.dynamic_slice_in_dim(p, me[0] * own, own, axis=1), (p.shape[0], own), lambda j, me: (0, 0)) for p in parts]
    return [(p, (p.shape[0], own), lambda j, me: (0, me[0])) for p in parts]


def view(ref, block, index):
    at = []
    for size, most, i in zip(block, ref.shape, index):
        start = i * size
        at.append(slice(None) if size == most else pl.ds(start if isinstance(start, int) else pl.multiple_of(start, size), size))
    return ref.at[tuple(at)]


def inside(count):
    return [pl.BlockSpec(memory_space=pltpu.VMEM)] * count


def local(kernel, name, arrays, outs, after=(), flops=0):
    skip = len(after)
    return pl.pallas_call(
        lambda *refs: kernel(*refs[skip:]),
        name=name,
        out_shape=[pltpu.VMEM(s, d) for s, d in outs],
        in_specs=[pl.BlockSpec(memory_space=pl.ANY)] * skip
        + inside(len(arrays)),
        out_specs=inside(len(outs)),
        compiler_params=pltpu.CompilerParams(vmem_limit_bytes=4 * MIB),
        cost_estimate=pl.CostEstimate(flops=flops, bytes_accessed=0, transcendentals=0),
    )(*after, *[pltpu.with_memory_space_constraint(a, pltpu.VMEM) for a in arrays])


def steps_body(kernel, steps, ins, outs, *refs):
    for j in range(steps):
        kernel(*[view(r, b, m(j)) for r, (b, m) in zip(refs, ins + outs)])


def call(kernel, name, steps, ins, outs, flops, scalars=(), resident=False, after=()):
    if resident:
        body = functools.partial(steps_body, kernel, steps, [i[1:] for i in ins], [o[2:] for o in outs])
        return local(body, name, [i[0] for i in ins], [o[:2] for o in outs], after, flops)
    moved = sum(math.prod(a.shape) * a.dtype.itemsize for a, _, _ in ins)
    moved += sum(math.prod(s) * jnp.dtype(d).itemsize for s, d, _, _ in outs)
    return pl.pallas_call(
        kernel,
        name=name,
        out_shape=[jax.ShapeDtypeStruct(s, d) for s, d, _, _ in outs],
        grid_spec=pltpu.PrefetchScalarGridSpec(
            num_scalar_prefetch=len(scalars),
            grid=(steps,),
            in_specs=[pl.BlockSpec(b, m) for _, b, m in ins],
            out_specs=[pl.BlockSpec(b, m) for _, _, b, m in outs],
        ),
        compiler_params=pltpu.CompilerParams(vmem_limit_bytes=32 * MIB),
        cost_estimate=pl.CostEstimate(flops=flops, bytes_accessed=moved, transcendentals=0),
    )(*scalars, *[i[0] for i in ins])


def load_kernel(count, *refs):
    sources, places, sems = refs[:count], refs[count:2 * count], refs[2 * count]
    copies = [pltpu.make_async_copy(sources[i], places[i], sems.at[i]) for i in range(count)]
    for copy in copies:
        copy.start()
    for copy in copies:
        copy.wait()


def load(arrays, after=()):
    count, skip = len(arrays), len(after)
    return pl.pallas_call(
        lambda *refs: load_kernel(count, *refs[skip:]),
        name="load",
        out_shape=[pltpu.VMEM(a.shape, a.dtype) for a in arrays],
        in_specs=[pl.BlockSpec(memory_space=pl.ANY)] * skip + [pl.BlockSpec(memory_space=pltpu.HBM)] * count,
        out_specs=inside(count),
        scratch_shapes=[pltpu.SemaphoreType.DMA((count,))],
        compiler_params=pltpu.CompilerParams(vmem_limit_bytes=MIB),
        cost_estimate=pl.CostEstimate(flops=0, bytes_accessed=0, transcendentals=0),
    )(*after, *[pltpu.with_memory_space_constraint(a, pltpu.HBM) for a in arrays])


def wide(ref):
    return ref[...].astype(jnp.float32)


def join_kernel(groups, *refs):
    ins, outs = refs[:sum(len(g) for g in groups)], refs[sum(len(g) for g in groups):]
    for group, out in zip(groups, outs):
        values = [wide(r)[start:start + count] for r, (start, count) in zip(ins, group)]
        out[...] = cat(values).astype(out.dtype)
        ins = ins[len(group):]


def join(lists, after=(), flops=0):
    lists = [[p if isinstance(p, tuple) else (p, 0, p.shape[0]) for p in parts] for parts in lists]
    outs = [((sum(c for _, _, c in parts), parts[0][0].shape[1]), parts[0][0].dtype) for parts in lists]
    kernel = functools.partial(join_kernel, [[p[1:] for p in parts] for parts in lists])
    return local(kernel, "join", [p[0] for parts in lists for p in parts], outs, after, flops)


def pair_kernel(keep, *refs):
    got, (low, high) = refs[:-2], refs[-2:]
    part = wide(keep) + cat([wide(g) for g in got])
    half = part.shape[0] // 2
    low[...] = part[:half]
    high[...] = part[half:].astype(high.dtype)


def line_kernel(n, low, got, *outs):
    part = low[...] + wide(got)
    for k, out in enumerate(outs):
        out[...] = part[(k + 1) * n:(k + 2) * n].astype(out.dtype)


def open_kernel(n, count, low, got, *refs):
    line_kernel(n, low, got, *refs[-2 - count:-2])
    pair_kernel(*refs[:-2 - count], *refs[-2:])


def error_kernel(n, low, got, *refs):
    refs, target, out = refs[:-2], refs[-2], refs[-1]
    value = low[:n] + wide(got)[:n]
    for r in refs:
        value = value + wide(r)[:n]
    out[...] = (value - wide(target)).astype(out.dtype)


def turn_kernel(n, count, low, got, *refs):
    ends, (target, next_low, next_got), outs = refs[:count], refs[count:count + 3], refs[count + 3:]
    error_kernel(n, low, got, *ends, target, outs[-1])
    part = next_low[...] + wide(next_got)
    for k, out in enumerate(outs[:-1]):
        out[...] = cat([part[(k + 1) * n:(k + 2) * n], wide(outs[-1])]).astype(out.dtype)


def encode_kernel(parts, *refs):
    x = cat([r[...] for r in refs[:parts]])
    w, b, pre, code = refs[parts:]
    value = jnp.maximum(dot(x, w[0], ((1,), (0,))) + b[0], 0.0)
    pre[...] = value
    code[...] = (0.5 * value * value).astype(code.dtype)


def encode(source, parts, weight, bias, resident, after=()):
    _, width, feats = weight.shape
    m = sum(p.shape[0] for p in parts)
    c = piece(feats, 256)
    ins = [(p, p.shape, lambda j: (0, 0)) for p in parts]
    ins.append((weight, (1, width, c), lambda j: (source, 0, j)))
    ins.append((bias, (1, 1, c), lambda j: (source, 0, j)))
    outs = [((m, feats), d, (m, c), lambda j: (0, j)) for d in (jnp.float32, jnp.bfloat16)]
    return call(
        functools.partial(encode_kernel, len(parts)), "encode", feats // c, ins, outs, 2 * m * width * feats, (), resident, after
    )


def decode_kernel(sources, early, last, *refs):
    total = refs[2 * sources][...] if early else None
    for s in range(sources):
        term = dot(refs[s][...], refs[sources + s][0], ((1,), (0,)))
        total = term if total is None else total + term
    if not last:
        refs[-1][...] = total
        return
    keep, *gives = refs[2 * sources + early:]
    half = keep.shape[0]
    keep[...] = total[:half].astype(keep.dtype)
    size = half // len(gives)
    for k, give in enumerate(gives):
        give[...] = total[half + k * size:half + (k + 1) * size].astype(give.dtype)


def decode(target, sources, codes, weight, layers, early, last, resident, after=(), pieces=1):
    _, feats, width = weight.shape
    m = codes[0].shape[0]
    c = piece(width, 768)
    ins = [(codes[s], codes[s].shape, lambda j: (0, 0)) for s in sources]
    for s in sources:
        slot = pair_slot(s, target, layers)
        ins.append((weight, (1, feats, c), lambda j, slot=slot: (slot, 0, j)))
    ins += [(e, (m, c), lambda j: (0, j)) for e in early]
    outs = [((r, width), jnp.bfloat16, (r, c), lambda j: (0, j)) for r in [m // 2] + [m // 2 // pieces] * pieces]
    if not last:
        outs = [((m, width), jnp.float32, (m, c), lambda j: (0, j))]
    return call(
        functools.partial(decode_kernel, len(sources), len(early), last),
        "decode",
        width // c,
        ins,
        outs,
        2 * m * width * feats * len(sources),
        (),
        resident,
        after,
    )


def some(part):
    return part if isinstance(part, tuple) else (part, 0, part.shape[0])


def back_kernel(layers, counts, parts, known, *refs):
    errors = []
    for count in counts:
        errors.append(cat([r[...] for r in refs[:count]]))
        refs = refs[count:]
    pre = []
    for _ in range(layers):
        pre.append(cat([r[...] for r in refs[:parts]]))
        refs = refs[parts:]
    pairs = layers * (layers + 1) // 2
    weight, refs = refs[:pairs], refs[pairs:]
    early, refs = refs[:known], refs[known:]
    out, total = refs[:layers], refs[layers]
    for s in range(layers):
        value = early[s][...] if s < known else None
        for t in range(max(s, layers - 1 if s < known else 0), layers):
            term = dot(errors[t], weight[pair_slot(s, t, layers)][0], ((1,), (1,)))
            value = term if value is None else value + term
        value = (value * pre[s]).astype(out[s].dtype)
        out[s][...] = value
        total[s] = jnp.sum(value.astype(jnp.float32), axis=0, keepdims=True)


def back(errors, pre, weight, layers, resident, early=(), after=()):
    pairs, feats, width = weight.shape
    errors, pre = ([[some(p) for p in parts] for parts in lists] for lists in (errors, pre))
    m = sum(count for _, _, count in pre[0])
    c = piece(feats, 256)
    ins = [(e, (r, width), lambda j, i=i // r: (i, 0)) for parts in errors for e, i, r in parts]
    ins += [(p, (r, c), lambda j, i=i // r: (i, j)) for parts in pre for p, i, r in parts]
    ins += [(weight, (1, c, width), lambda j, k=k: (k, j, 0)) for k in range(pairs)]
    ins += [(e, (m, c), lambda j: (0, j)) for e in early]
    outs = [((m, feats), jnp.bfloat16, (m, c), lambda j: (0, j))] * layers
    outs.append(((layers, 1, feats), jnp.float32, (layers, 1, c), lambda j: (0, 0, j)))
    got = call(
        functools.partial(back_kernel, layers, [len(e) for e in errors], len(pre[0]), len(early)),
        "back",
        feats // c,
        ins,
        outs,
        2 * m * width * feats * (pairs - len(early)),
        (),
        resident,
        after,
    )
    return got[:layers], got[layers]


def first_kernel(parts, *refs):
    error = cat([r[...] for r in refs[:parts]])
    weight, out = refs[parts:]
    out[...] = dot(error, weight[0], ((1,), (1,)))


def first(errors, weight, after=()):
    _, feats, width = weight.shape
    m = sum(e.shape[0] for e in errors)
    c = piece(feats, 256)
    ins = [(e, e.shape, lambda j: (0, 0)) for e in errors]
    ins.append((weight, (1, c, width), lambda j: (0, j, 0)))
    outs = [((m, feats), jnp.float32, (m, c), lambda j: (0, j))]
    body = functools.partial(first_kernel, len(errors))
    return call(body, "first", feats // c, ins, outs, 2 * m * width * feats, (), True, after)[0]


def dec_kernel(layers, scale, counts, me, *refs):
    a, b = counts
    codes = [cat([r[...] for r in refs[s * a:(s + 1) * a]]) for s in range(layers)]
    refs = refs[layers * a:]
    errors = [cat([r[...] for r in refs[t * b:(t + 1) * b]]) for t in range(layers)]
    out = refs[layers * b]
    for s in range(layers):
        for t in range(s, layers):
            value = dot(codes[s], errors[t], ((0,), (0,))) * scale
            out[pair_slot(s, t, layers)] = value.astype(out.dtype)


def dec_grads(codes, errors, me, own, scale, layers):
    width = errors[0][0].shape[1]
    pairs = layers * (layers + 1) // 2
    m = sum(p.shape[0] for p in codes[0])
    c = piece(width, 768)
    ins = [i for s in range(layers) for i in share(codes[s], own, me)]
    ins += [(p, (p.shape[0], c), lambda j, me: (0, j)) for t in range(layers) for p in errors[t]]
    outs = [((pairs, own, width), jnp.bfloat16, (pairs, own, c), lambda j, me: (0, 0, j))]
    return call(
        functools.partial(dec_kernel, layers, scale, (len(codes[0]), len(errors[0]))),
        "dec_grads",
        width // c,
        ins,
        outs,
        2 * m * width * own * pairs,
        (me,),
    )[0]


def enc_kernel(layers, scale, counts, me, *refs):
    a, b = counts
    inputs = [cat([r[...] for r in refs[s * a:(s + 1) * a]]) for s in range(layers)]
    refs = refs[layers * a:]
    grads = [cat([r[...] for r in refs[s * b:(s + 1) * b]]) for s in range(layers)]
    out = refs[layers * b]
    for s in range(layers):
        out[s] = (dot(inputs[s], grads[s], ((0,), (0,))) * scale).astype(out.dtype)


def enc_grads(inputs, grads, me, own, scale, layers):
    feats = grads[0][0].shape[1]
    m = sum(p.shape[0] for p in inputs[0])
    c = piece(feats, 256)
    ins = [i for s in range(layers) for i in share(inputs[s], own, me)]
    ins += [(p, (p.shape[0], c), lambda j, me: (0, j)) for s in range(layers) for p in grads[s]]
    outs = [((layers, own, feats), jnp.bfloat16, (layers, own, c), lambda j, me: (0, 0, j))]
    return call(
        functools.partial(enc_kernel, layers, scale, (len(inputs[0]), len(grads[0]))),
        "enc_grads",
        feats // c,
        ins,
        outs,
        2 * m * own * feats * layers,
        (me,),
    )[0]


def mine(size):
    return pl.ds(pl.multiple_of(lax.axis_index("tok") * size, 128), size)


def gathered(parts, size):
    at = slice(None) if parts[0][0].shape[1] == size else mine(size)
    return cat([p[start:start + count, at] for p, (start, count) in parts])


def ahead_kernel(rows, own, *refs):
    *ins, out = refs
    count = len(rows[0])
    left = gathered(list(zip(ins[:count], rows[0])), own)
    right = gathered(list(zip(ins[count:], rows[1])), out.shape[1])
    size = piece(right.shape[1], 768)
    for j in range(right.shape[1] // size):
        at = slice(j * size, (j + 1) * size)
        out[:, at] = dot(left, right[:, at], ((0,), (0,)))


def ahead(codes, errors, own):
    lists = [[some(p) for p in parts] for parts in (codes, errors)]
    rows = [[p[1:] for p in parts] for parts in lists]
    arrays = [p[0] for parts in lists for p in parts]
    out = ((own, arrays[-1].shape[1]), jnp.float32)
    flops = 2 * math.prod(out[0]) * sum(r[1] for r in rows[0])
    return local(functools.partial(ahead_kernel, rows, own), "ahead", arrays, [out], (), flops)[0]


def grads_body(layers, scale, rows, own, late, *refs):
    lists = []
    for parts in rows:
        lists.append([])
        for bounds in parts:
            lists[-1].append(list(zip(refs, bounds)))
            refs = refs[len(bounds):]
    codes, errors, inputs, grads = lists
    early, sums, refs = refs[0], refs[1:-7], refs[-7:]
    dec_out, enc_out, bias_out, dec_held, enc_held, dec_sems, enc_sems = refs
    copies = []
    def leave(held, out, sems, slot, left, right, before=None):
        width = right.shape[1]
        size = piece(width, 768)
        for j in range(width // size):
            value = dot(left, right[:, j * size:(j + 1) * size], ((0,), (0,)))
            if before is not None:
                value = value + before[:, j * size:(j + 1) * size]
            at = (slot, slice(None), slice(j * size, (j + 1) * size))
            held[at] = (value * scale).astype(held.dtype)
            copy = pltpu.make_async_copy(held.at[at], out.at[at], sems.at[slot, j])
            copy.start()
            copies.append(copy)

    for s in range(layers):
        left = gathered(codes[s], own[0])
        for t in range(s, layers):
            slot, before, first = pair_slot(s, t, layers), None, left
            right = errors[t]
            if slot == 0:
                before, first, right = early, gathered(codes[s][-late:], own[0]), right[-late:]
            leave(dec_held, dec_out, dec_sems, slot, first, gathered(right, dec_out.shape[2]), before)
    for s in range(layers):
        leave(enc_held, enc_out, enc_sems, s, gathered(inputs[s], own[1]), gathered(grads[s], enc_out.shape[2]))
        total = sums[0][s, :, mine(own[0])]
        for more in sums[1:]:
            total = total + more[s, :, mine(own[0])]
        bias_out[pl.ds(s, 1)] = total * scale
    for copy in copies:
        copy.wait()


def all_grads(codes, errors, inputs, grads, early, late, sums, own, scale, layers):
    lists = [[[some(p) for p in parts] for parts in each] for each in (codes, errors, inputs, grads)]
    rows = [[[p[1:] for p in parts] for parts in each] for each in lists]
    dec = (layers * (layers + 1) // 2, own[0], lists[1][0][0][0].shape[1])
    enc = (layers, own[1], lists[3][0][0][0].shape[1])
    arrays = [p[0] for each in lists for parts in each for p in parts] + [early, *sums]
    arrays = [pltpu.with_memory_space_constraint(a, pltpu.VMEM) for a in arrays]
    return pl.pallas_call(
        functools.partial(grads_body, layers, scale, rows, own, late),
        name="grads",
        out_shape=[
            jax.ShapeDtypeStruct(dec, jnp.bfloat16),
            jax.ShapeDtypeStruct(enc, jnp.bfloat16),
            jax.ShapeDtypeStruct((layers, own[0]), jnp.float32),
        ],
        in_specs=inside(len(arrays)),
        out_specs=[pl.BlockSpec(memory_space=pltpu.HBM)] * 2 + inside(1),
        scratch_shapes=[
            pltpu.VMEM(dec, jnp.bfloat16),
            pltpu.VMEM(enc, jnp.bfloat16),
            pltpu.SemaphoreType.DMA((dec[0], dec[2] // piece(dec[2], 768))),
            pltpu.SemaphoreType.DMA((enc[0], enc[2] // piece(enc[2], 768))),
        ],
        compiler_params=pltpu.CompilerParams(vmem_limit_bytes=2 * (math.prod(dec) + math.prod(enc)) + 8 * MIB),
        cost_estimate=pl.CostEstimate(flops=0, bytes_accessed=0, transcendentals=0),
    )(*arrays)


def plain(acts_in, targets, enc_weight, bias, dec_weight, scale):
    layers, width, feats = enc_weight.shape
    feat, tok = lax.axis_size("feat"), lax.axis_size("tok")

    def gather(value):
        return lax.all_gather(value, "feat", axis=0, tiled=True)

    inputs, pre, codes, errors, grads, sums = [], [], [], [], [], []
    for g in range(tok):
        acts = swap(acts_in, "tok", g) if g else acts_in
        inputs.append([])
        pre.append([])
        codes.append([])
        for s in range(layers):
            inputs[g].append([gather(acts[:, s, :])])
            p, c = encode(s, inputs[g][s], enc_weight, bias, False)
            pre[g].append(p)
            codes[g].append(c)
    own = []
    for t in range(layers):
        halves = decode(t, range(t + 1), codes[0], dec_weight, layers, (), True, False)
        part = lax.psum_scatter(cat(halves), "feat", scatter_dimension=0, tiled=True)
        own.append((part.astype(jnp.float32) - targets[:, t, :].astype(jnp.float32)).astype(jnp.bfloat16))
    for g in range(tok):
        errors.append([[gather(swap(e, "tok", g) if g else e)] for e in own])
        d, total = back(errors[g], [[p] for p in pre[g]], dec_weight, layers, False)
        grads.append(d)
        sums.append(total)
    me = lax.axis_index("tok")
    index = me.reshape(1).astype(jnp.int32)

    def every(parts):
        return [[parts[g][s] for g in range(tok)] for s in range(layers)]

    def flat(parts):
        return [[parts[g][s][0] for g in range(tok)] for s in range(layers)]

    rows = feats // tok
    dec_out = dec_grads(every(codes), flat(errors), index, rows, scale, layers)
    enc_out = enc_grads(flat(inputs), every(grads), index, width // tok, scale, layers)
    total = sum(sums[1:], sums[0]).reshape(layers, feats) * scale
    return enc_out, lax.dynamic_slice_in_dim(total, me * rows, rows, axis=1), dec_out


def staged(acts_in, targets, enc_weight, bias, dec_weight, scale):
    layers, width, feats = enc_weight.shape
    n = acts_in.shape[0]
    quart = n * (lax.axis_size("feat") // 4)
    hop = quart // 2
    line = [4 * k for k in range(1, lax.axis_size("feat") // 4)]
    small = ((n, width), jnp.bfloat16)
    lows = [((quart, width), jnp.float32), ((quart, width), jnp.bfloat16)]

    def along(values):
        return [swap(v, "feat", bits) for v, bits in zip(values, line)]

    def across(value):
        return swap(value, "feat", 2)

    def core(value):
        return swap(value, "feat", 1)

    def away(value):
        return swap(value, "tok", 1)

    def encoded(s, parts, after=()):
        return encode(s, parts, enc_held, bias, True, after)

    def pair(keep, got, after):
        return local(pair_kernel, "pair", [keep, *got], lows, after)

    def error(low, got, ends, target, after):
        arrays = [low, got, *ends, target]
        return local(functools.partial(error_kernel, n), "error", arrays, [small], after)[0]

    def nears(parts):
        return [(p, 0, quart) for p in parts]

    def fars(parts):
        return [(p, quart, quart) for p in parts]

    def halves(value):
        return [(value, k * quart, quart) for k in (0, 2)], [(value, k * quart, quart) for k in (1, 3)]

    acts = [acts_in[:, 0, :]]
    ends = quart - n
    z_a0 = along([acts[0]] * len(line))
    enc_held = load([enc_weight])[0]
    acts.append(lax.optimization_barrier((acts_in, enc_held))[0][:, 1, :])
    done = [*z_a0, enc_held]
    line0, send, a1 = join([z_a0, [*z_a0, *acts], [acts[1]]], done)
    y_s, x_s = away(send), across(send)
    z_a1 = along([a1] * len(line))
    dec_held = load([dec_weight], [line0])[0]
    done = [*z_a1, x_s, y_s, dec_held]
    far0, far1 = [(x_s, ends, n), (x_s, 0, ends)], [(x_s, quart, n)]
    line1, col0 = join([z_a1, [acts[0], line0, *far0]], done)
    x_l1 = across(line1)
    in0 = [col0, core(col0)]
    pre0, code0 = encoded(0, in0)
    keep0, *give0 = decode(0, [0], [code0], dec_held, layers, (), True, True, (), 3)
    got0 = [core(g) for g in give0]
    done = [x_l1, *got0]
    low0, high0 = pair(keep0, got0, done)
    far1.append(x_l1)
    col1, far_both = join([[a1, line1, *far1], far0 + far1], [*done, high0])
    y_l1, x_h0 = away(line1), across(high0)
    in1 = [col1, core(col1)]
    early = decode(1, [0], [code0], dec_held, layers, (), False, True, (low0, col1))
    pre1, code1 = encoded(1, in1, early)
    keep1, *give1 = decode(1, [1], [code0, code1], dec_held, layers, early, True, True, (), 3)
    got1 = [core(g) for g in give1]
    done = [x_h0, y_l1, *got1]
    body = functools.partial(open_kernel, n, len(line))
    *ends0, low1, high1 = local(body, "open", [low0, x_h0, keep1, *got1], [small] * len(line) + lows, done)
    z_r0 = along(ends0)
    x_h1 = across(high1)
    done = [*z_r0, x_h1]
    target0, target1 = join([[targets[:, 0, :]], [targets[:, 1, :]]], [low1], 2 * quart * width * feats)
    arrays = [low0, x_h0, *z_r0, target0, low1, x_h1]
    shapes = [((2 * n, width), jnp.bfloat16)] * len(line) + [small]
    *turned, e0 = local(functools.partial(turn_kernel, n, len(line)), "turn", arrays, shapes, done)
    y_f, y_e0, x_e0 = away(far_both), away(e0), across(e0)
    z_t = along(turned)
    done = [*z_t, x_e0, y_e0, y_f]
    e1 = error(low1, x_h1, z_t, target1, done)
    lines = [(z, n, n) for z in z_t]
    near0, both = join([[e0, *lines], [*lines, e1]], done)
    there0 = [(y_s, ends, n), (y_s, 0, ends), (y_f, 0, quart)]
    there0, there1 = join([there0, [(y_s, quart, n), y_l1, (y_f, quart, quart)]], [*done, both])
    y_b, x_b = away(both), across(both)
    z_e1 = along([e1] * len(line))
    there_in0, there_in1 = [there0, core(there0)], [there1, core(there1)]
    there_pre0, there_code0 = encoded(0, there_in0)
    there_pre1, there_code1 = encoded(1, there_in1)
    done = [*z_e1, x_b, y_b, there_code0, there_code1]
    near1, send = join([[e1, *z_e1], z_e1], (), 32 * quart * width * feats)
    whole0, near_y0 = join(
        [[near0, x_e0, (x_b, 0, ends)], [y_e0, (y_b, 0, ends)]], [there_code0, there_code1]
    )
    y_g, x_g = away(send), across(send)
    err0 = [whole0, core(whole0)]
    near_err0 = [near_y0, core(near_y0)]
    first_own = first(err0, dec_held)
    first_near = first(near_err0, dec_held)
    share = (feats // lax.axis_size("tok"), width // lax.axis_size("tok"))
    early = ahead([code0] + halves(there_code0)[0], err0 + near_err0, share[0])
    done = [x_g, y_g, first_own, first_near]
    whole1, near_y1, go_x, go_y = join(
        [
            [near1, (x_b, ends, n), x_g],
            [(y_b, ends, n), y_g],
            [(near_y0, 0, hop), (y_b, ends, n), (y_g, 0, hop - n)],
            [(x_b, hop - n, quart - hop), (x_g, hop - n, quart - hop)],
        ],
        done,
    )
    y_t, x_o = away(go_y), across(go_x)
    err1 = [whole1, core(whole1)]
    near_err1 = [near_y1, core(near_y1)]

    near_pre, far_pre = zip(halves(there_pre0), halves(there_pre1))
    grad_own, sum_own = back([err0, err1], [[pre0], [pre1]], dec_held, layers, True, [first_own])
    grad_near, sum_near = back([near_err0, near_err1], near_pre, dec_held, layers, True, [first_near])
    done = [x_o, y_t, grad_own[0], grad_near[0], early]
    left = quart - hop
    far0, far1 = join([[(x_o, 0, hop), (y_t, 0, left)], [(x_o, hop, hop), (y_t, left, left)]], done)
    far_errs = [[far0, core(far0)], [far1, core(far1)]]
    grad_far, sum_far = back(far_errs, far_pre, dec_held, layers, True)
    codes = [sum(halves(c), []) for c in (there_code0, there_code1)]
    seen = [nears(p) + fars(p) for p in (there_in0, there_in1)]
    dec_out, enc_out, bias_out = all_grads(
        [[code0] + codes[0], [code1] + codes[1]],
        [err0 + near_err0 + far_errs[0], err1 + near_err1 + far_errs[1]],
        [in0 + seen[0], in1 + seen[1]],
        [[grad_own[s], grad_near[s], grad_far[s]] for s in range(layers)],
        early,
        2,
        [sum_own, sum_near, sum_far],
        share,
        scale,
        layers,
    )
    return enc_out, bias_out, dec_out


def shards(acts_in, targets, enc_weight, enc_bias, dec_weight):
    layers, width, feats = enc_weight.shape
    n = acts_in.shape[0]
    feat, tok = lax.axis_size("feat"), lax.axis_size("tok")
    scale = 1.0 / math.sqrt(n * feat * tok)
    bias = enc_bias.reshape(layers, 1, feats)
    held = 2 * (math.prod(enc_weight.shape) + math.prod(dec_weight.shape))
    held += 4 * layers * n * feat * tok * (width + 2 * feats)
    fits = held <= 54 * MIB and n % 8 == 0 and (feats // tok) % 128 == 0 and (width // tok) % 128 == 0
    run = staged if fits and layers == 2 and tok == 2 and feat >= 8 else plain
    return run(acts_in, targets, enc_weight, bias, dec_weight, scale)


def solution(mesh):
    return jax.shard_map(
        shards,
        mesh=mesh,
        in_specs=(
            P(("tok", "feat"), None, None),
            P(("tok", "feat"), None, None),
            P(None, None, "feat"),
            P(None, "feat"),
            P(None, "feat", None),
        ),
        out_specs=(
            P(None, "tok", "feat"),
            P(None, ("feat", "tok")),
            P(None, ("feat", "tok"), None),
        ),
        check_vma=False,
    )
```

```python
import functools
import math

import jax
import jax.numpy as jnp
from jax import lax
from jax.experimental import pallas as pl
from jax.experimental.pallas import tpu as pltpu
from jax.sharding import PartitionSpec as P

MIB = 1 << 20


def pair_slot(source, target, layers):
    return sum((layers - k for k in range(source))) + (target - source)


def swap(value, axis, bits):
    return lax.ppermute(value, axis, [(i, i ^ bits) for i in range(lax.axis_size(axis))])


def cat(parts):
    return parts[0] if len(parts) == 1 else jnp.concatenate(parts, axis=0)


def dot(a, b, dims):
    return lax.dot_general(a, b, (dims, ((), ())), preferred_element_type=jnp.float32)


def piece(size, most):
    for c in range(most - most % 128, 0, -128):
        if size % c == 0:
            return c
    return size


def share(parts, own, me):
    if own % 128:
        return [(lax.dynamic_slice_in_dim(p, me[0] * own, own, axis=1), (p.shape[0], own), lambda j, me: (0, 0)) for p in parts]
    return [(p, (p.shape[0], own), lambda j, me: (0, me[0])) for p in parts]


def view(ref, block, index):
    at = []
    for size, most, i in zip(block, ref.shape, index):
        start = i * size
        at.append(slice(None) if size == most else pl.ds(start if isinstance(start, int) else pl.multiple_of(start, size), size))
    return ref.at[tuple(at)]


def inside(count):
    return [pl.BlockSpec(memory_space=pltpu.VMEM)] * count


def local(kernel, name, arrays, outs, after=(), flops=0):
    skip = len(after)
    return pl.pallas_call(
        lambda *refs: kernel(*refs[skip:]),
        name=name,
        out_shape=[pltpu.VMEM(s, d) for s, d in outs],
        in_specs=[pl.BlockSpec(memory_space=pl.ANY)] * skip
        + inside(len(arrays)),
        out_specs=inside(len(outs)),
        compiler_params=pltpu.CompilerParams(vmem_limit_bytes=4 * MIB),
        cost_estimate=pl.CostEstimate(flops=flops, bytes_accessed=0, transcendentals=0),
    )(*after, *[pltpu.with_memory_space_constraint(a, pltpu.VMEM) for a in arrays])


def steps_body(kernel, steps, ins, outs, *refs):
    for j in range(steps):
        kernel(*[view(r, b, m(j)) for r, (b, m) in zip(refs, ins + outs)])


def call(kernel, name, steps, ins, outs, flops, scalars=(), resident=False, after=()):
    if resident:
        body = functools.partial(steps_body, kernel, steps, [i[1:] for i in ins], [o[2:] for o in outs])
        return local(body, name, [i[0] for i in ins], [o[:2] for o in outs], after, flops)
    moved = sum(math.prod(a.shape) * a.dtype.itemsize for a, _, _ in ins)
    moved += sum(math.prod(s) * jnp.dtype(d).itemsize for s, d, _, _ in outs)
    return pl.pallas_call(
        kernel,
        name=name,
        out_shape=[jax.ShapeDtypeStruct(s, d) for s, d, _, _ in outs],
        grid_spec=pltpu.PrefetchScalarGridSpec(
            num_scalar_prefetch=len(scalars),
            grid=(steps,),
            in_specs=[pl.BlockSpec(b, m) for _, b, m in ins],
            out_specs=[pl.BlockSpec(b, m) for _, _, b, m in outs],
        ),
        compiler_params=pltpu.CompilerParams(vmem_limit_bytes=32 * MIB),
        cost_estimate=pl.CostEstimate(flops=flops, bytes_accessed=moved, transcendentals=0),
    )(*scalars, *[i[0] for i in ins])


def load_kernel(count, *refs):
    sources, places, sems = refs[:count], refs[count:2 * count], refs[2 * count]
    copies = [pltpu.make_async_copy(sources[i], places[i], sems.at[i]) for i in range(count)]
    for copy in copies:
        copy.start()
    for copy in copies:
        copy.wait()


def load(arrays, after=()):
    count, skip = len(arrays), len(after)
    return pl.pallas_call(
        lambda *refs: load_kernel(count, *refs[skip:]),
        name="load",
        out_shape=[pltpu.VMEM(a.shape, a.dtype) for a in arrays],
        in_specs=[pl.BlockSpec(memory_space=pl.ANY)] * skip + [pl.BlockSpec(memory_space=pltpu.HBM)] * count,
        out_specs=inside(count),
        scratch_shapes=[pltpu.SemaphoreType.DMA((count,))],
        compiler_params=pltpu.CompilerParams(vmem_limit_bytes=MIB),
        cost_estimate=pl.CostEstimate(flops=0, bytes_accessed=0, transcendentals=0),
    )(*after, *[pltpu.with_memory_space_constraint(a, pltpu.HBM) for a in arrays])


def wide(ref):
    return ref[...].astype(jnp.float32)


def join_kernel(groups, *refs):
    ins, outs = refs[:sum(len(g) for g in groups)], refs[sum(len(g) for g in groups):]
    for group, out in zip(groups, outs):
        values = [wide(r)[start:start + count] for r, (start, count) in zip(ins, group)]
        out[...] = cat(values).astype(out.dtype)
        ins = ins[len(group):]


def join(lists, after=(), flops=0):
    lists = [[p if isinstance(p, tuple) else (p, 0, p.shape[0]) for p in parts] for parts in lists]
    outs = [((sum(c for _, _, c in parts), parts[0][0].shape[1]), parts[0][0].dtype) for parts in lists]
    kernel = functools.partial(join_kernel, [[p[1:] for p in parts] for parts in lists])
    return local(kernel, "join", [p[0] for parts in lists for p in parts], outs, after, flops)


def pair_kernel(keep, *refs):
    got, (low, high) = refs[:-2], refs[-2:]
    part = wide(keep) + cat([wide(g) for g in got])
    half = part.shape[0] // 2
    low[...] = part[:half]
    high[...] = part[half:].astype(high.dtype)


def line_kernel(n, low, got, *outs):
    part = low[...] + wide(got)
    for k, out in enumerate(outs):
        out[...] = part[(k + 1) * n:(k + 2) * n].astype(out.dtype)


def open_kernel(n, count, low, got, *refs):
    line_kernel(n, low, got, *refs[-2 - count:-2])
    pair_kernel(*refs[:-2 - count], *refs[-2:])


def error_kernel(n, low, got, *refs):
    refs, target, out = refs[:-2], refs[-2], refs[-1]
    value = low[:n] + wide(got)[:n]
    for r in refs:
        value = value + wide(r)[:n]
    out[...] = (value - wide(target)).astype(out.dtype)


def turn_kernel(n, count, low, got, *refs):
    ends, (target, next_low, next_got), outs = refs[:count], refs[count:count + 3], refs[count + 3:]
    error_kernel(n, low, got, *ends, target, outs[-1])
    part = next_low[...] + wide(next_got)
    for k, out in enumerate(outs[:-1]):
        out[...] = cat([part[(k + 1) * n:(k + 2) * n], wide(outs[-1])]).astype(out.dtype)


def encode_kernel(parts, *refs):
    x = cat([r[...] for r in refs[:parts]])
    w, b, pre, code = refs[parts:]
    value = jnp.maximum(dot(x, w[0], ((1,), (0,))) + b[0], 0.0)
    pre[...] = value
    code[...] = (0.5 * value * value).astype(code.dtype)


def encode(source, parts, weight, bias, resident, after=()):
    _, width, feats = weight.shape
    m = sum(p.shape[0] for p in parts)
    c = piece(feats, 256)
    ins = [(p, p.shape, lambda j: (0, 0)) for p in parts]
    ins.append((weight, (1, width, c), lambda j: (source, 0, j)))
    ins.append((bias, (1, 1, c), lambda j: (source, 0, j)))
    outs = [((m, feats), d, (m, c), lambda j: (0, j)) for d in (jnp.float32, jnp.bfloat16)]
    return call(
        functools.partial(encode_kernel, len(parts)), "encode", feats // c, ins, outs, 2 * m * width * feats, (), resident, after
    )


def decode_kernel(sources, early, last, *refs):
    total = refs[2 * sources][...] if early else None
    for s in range(sources):
        term = dot(refs[s][...], refs[sources + s][0], ((1,), (0,)))
        total = term if total is None else total + term
    if not last:
        refs[-1][...] = total
        return
    keep, *gives = refs[2 * sources + early:]
    half = keep.shape[0]
    keep[...] = total[:half].astype(keep.dtype)
    size = half // len(gives)
    for k, give in enumerate(gives):
        give[...] = total[half + k * size:half + (k + 1) * size].astype(give.dtype)


def decode(target, sources, codes, weight, layers, early, last, resident, after=(), pieces=1):
    _, feats, width = weight.shape
    m = codes[0].shape[0]
    c = piece(width, 768)
    ins = [(codes[s], codes[s].shape, lambda j: (0, 0)) for s in sources]
    for s in sources:
        slot = pair_slot(s, target, layers)
        ins.append((weight, (1, feats, c), lambda j, slot=slot: (slot, 0, j)))
    ins += [(e, (m, c), lambda j: (0, j)) for e in early]
    outs = [((r, width), jnp.bfloat16, (r, c), lambda j: (0, j)) for r in [m // 2] + [m // 2 // pieces] * pieces]
    if not last:
        outs = [((m, width), jnp.float32, (m, c), lambda j: (0, j))]
    return call(
        functools.partial(decode_kernel, len(sources), len(early), last),
        "decode",
        width // c,
        ins,
        outs,
        2 * m * width * feats * len(sources),
        (),
        resident,
        after,
    )


def some(part):
    return part if isinstance(part, tuple) else (part, 0, part.shape[0])


def back_kernel(layers, counts, parts, known, *refs):
    errors = []
    for count in counts:
        errors.append(cat([r[...] for r in refs[:count]]))
        refs = refs[count:]
    pre = []
    for _ in range(layers):
        pre.append(cat([r[...] for r in refs[:parts]]))
        refs = refs[parts:]
    pairs = layers * (layers + 1) // 2
    weight, refs = refs[:pairs], refs[pairs:]
    early, refs = refs[:known], refs[known:]
    out, total = refs[:layers], refs[layers]
    for s in range(layers):
        value = early[s][...] if s < known else None
        for t in range(max(s, layers - 1 if s < known else 0), layers):
            term = dot(errors[t], weight[pair_slot(s, t, layers)][0], ((1,), (1,)))
            value = term if value is None else value + term
        value = (value * pre[s]).astype(out[s].dtype)
        out[s][...] = value
        total[s] = jnp.sum(value.astype(jnp.float32), axis=0, keepdims=True)


def back(errors, pre, weight, layers, resident, early=(), after=()):
    pairs, feats, width = weight.shape
    errors, pre = ([[some(p) for p in parts] for parts in lists] for lists in (errors, pre))
    m = sum(count for _, _, count in pre[0])
    c = piece(feats, 256)
    ins = [(e, (r, width), lambda j, i=i // r: (i, 0)) for parts in errors for e, i, r in parts]
    ins += [(p, (r, c), lambda j, i=i // r: (i, j)) for parts in pre for p, i, r in parts]
    ins += [(weight, (1, c, width), lambda j, k=k: (k, j, 0)) for k in range(pairs)]
    ins += [(e, (m, c), lambda j: (0, j)) for e in early]
    outs = [((m, feats), jnp.bfloat16, (m, c), lambda j: (0, j))] * layers
    outs.append(((layers, 1, feats), jnp.float32, (layers, 1, c), lambda j: (0, 0, j)))
    got = call(
        functools.partial(back_kernel, layers, [len(e) for e in errors], len(pre[0]), len(early)),
        "back",
        feats // c,
        ins,
        outs,
        2 * m * width * feats * (pairs - len(early)),
        (),
        resident,
        after,
    )
    return got[:layers], got[layers]


def first_kernel(parts, *refs):
    error = cat([r[...] for r in refs[:parts]])
    weight, out = refs[parts:]
    out[...] = dot(error, weight[0], ((1,), (1,)))


def first(errors, weight, after=()):
    _, feats, width = weight.shape
    m = sum(e.shape[0] for e in errors)
    c = piece(feats, 256)
    ins = [(e, e.shape, lambda j: (0, 0)) for e in errors]
    ins.append((weight, (1, c, width), lambda j: (0, j, 0)))
    outs = [((m, feats), jnp.float32, (m, c), lambda j: (0, j))]
    body = functools.partial(first_kernel, len(errors))
    return call(body, "first", feats // c, ins, outs, 2 * m * width * feats, (), True, after)[0]


def dec_kernel(layers, scale, counts, me, *refs):
    a, b = counts
    codes = [cat([r[...] for r in refs[s * a:(s + 1) * a]]) for s in range(layers)]
    refs = refs[layers * a:]
    errors = [cat([r[...] for r in refs[t * b:(t + 1) * b]]) for t in range(layers)]
    out = refs[layers * b]
    for s in range(layers):
        for t in range(s, layers):
            value = dot(codes[s], errors[t], ((0,), (0,))) * scale
            out[pair_slot(s, t, layers)] = value.astype(out.dtype)


def dec_grads(codes, errors, me, own, scale, layers):
    width = errors[0][0].shape[1]
    pairs = layers * (layers + 1) // 2
    m = sum(p.shape[0] for p in codes[0])
    c = piece(width, 768)
    ins = [i for s in range(layers) for i in share(codes[s], own, me)]
    ins += [(p, (p.shape[0], c), lambda j, me: (0, j)) for t in range(layers) for p in errors[t]]
    outs = [((pairs, own, width), jnp.bfloat16, (pairs, own, c), lambda j, me: (0, 0, j))]
    return call(
        functools.partial(dec_kernel, layers, scale, (len(codes[0]), len(errors[0]))),
        "dec_grads",
        width // c,
        ins,
        outs,
        2 * m * width * own * pairs,
        (me,),
    )[0]


def enc_kernel(layers, scale, counts, me, *refs):
    a, b = counts
    inputs = [cat([r[...] for r in refs[s * a:(s + 1) * a]]) for s in range(layers)]
    refs = refs[layers * a:]
    grads = [cat([r[...] for r in refs[s * b:(s + 1) * b]]) for s in range(layers)]
    out = refs[layers * b]
    for s in range(layers):
        out[s] = (dot(inputs[s], grads[s], ((0,), (0,))) * scale).astype(out.dtype)


def enc_grads(inputs, grads, me, own, scale, layers):
    feats = grads[0][0].shape[1]
    m = sum(p.shape[0] for p in inputs[0])
    c = piece(feats, 256)
    ins = [i for s in range(layers) for i in share(inputs[s], own, me)]
    ins += [(p, (p.shape[0], c), lambda j, me: (0, j)) for s in range(layers) for p in grads[s]]
    outs = [((layers, own, feats), jnp.bfloat16, (layers, own, c), lambda j, me: (0, 0, j))]
    return call(
        functools.partial(enc_kernel, layers, scale, (len(inputs[0]), len(grads[0]))),
        "enc_grads",
        feats // c,
        ins,
        outs,
        2 * m * own * feats * layers,
        (me,),
    )[0]


def mine(size):
    return pl.ds(pl.multiple_of(lax.axis_index("tok") * size, 128), size)


def gathered(parts, size):
    at = slice(None) if parts[0][0].shape[1] == size else mine(size)
    return cat([p[start:start + count, at] for p, (start, count) in parts])


def ahead_kernel(rows, own, *refs):
    *ins, out = refs
    count = len(rows[0])
    left = gathered(list(zip(ins[:count], rows[0])), own)
    right = gathered(list(zip(ins[count:], rows[1])), out.shape[1])
    size = piece(right.shape[1], 768)
    for j in range(right.shape[1] // size):
        at = slice(j * size, (j + 1) * size)
        out[:, at] = dot(left, right[:, at], ((0,), (0,)))


def ahead(codes, errors, own, after=()):
    lists = [[some(p) for p in parts] for parts in (codes, errors)]
    rows = [[p[1:] for p in parts] for parts in lists]
    arrays = [p[0] for parts in lists for p in parts]
    out = ((own, arrays[-1].shape[1]), jnp.float32)
    flops = 2 * math.prod(out[0]) * sum(r[1] for r in rows[0])
    return local(functools.partial(ahead_kernel, rows, own), "ahead", arrays, [out], after, flops)[0]


def grads_body(layers, scale, rows, own, late, *refs):
    lists = []
    for parts in rows:
        lists.append([])
        for bounds in parts:
            lists[-1].append(list(zip(refs, bounds)))
            refs = refs[len(bounds):]
    codes, errors, inputs, grads = lists
    early, sums, refs = refs[:layers], refs[layers:-7], refs[-7:]
    dec_out, enc_out, bias_out, dec_held, enc_held, dec_sems, enc_sems = refs
    copies = []
    def leave(held, out, sems, slot, left, right, before=None):
        width = right.shape[1]
        size = piece(width, 768)
        for j in range(width // size):
            value = dot(left, right[:, j * size:(j + 1) * size], ((0,), (0,)))
            if before is not None:
                value = value + before[:, j * size:(j + 1) * size]
            at = (slot, slice(None), slice(j * size, (j + 1) * size))
            held[at] = (value * scale).astype(held.dtype)
            copy = pltpu.make_async_copy(held.at[at], out.at[at], sems.at[slot, j])
            copy.start()
            copies.append(copy)

    for s in range(layers):
        left = gathered(codes[s], own[0])
        for t in range(s, layers):
            slot, before, first = pair_slot(s, t, layers), None, left
            right = errors[t]
            if s == 0:
                before, first, right = early[t], gathered(codes[s][-late:], own[0]), right[-late:]
            leave(dec_held, dec_out, dec_sems, slot, first, gathered(right, dec_out.shape[2]), before)
    for s in range(layers):
        leave(enc_held, enc_out, enc_sems, s, gathered(inputs[s], own[1]), gathered(grads[s], enc_out.shape[2]))
        total = sums[0][s, :, mine(own[0])]
        for more in sums[1:]:
            total = total + more[s, :, mine(own[0])]
        bias_out[pl.ds(s, 1)] = total * scale
    for copy in copies:
        copy.wait()


def all_grads(codes, errors, inputs, grads, early, late, sums, own, scale, layers):
    lists = [[[some(p) for p in parts] for parts in each] for each in (codes, errors, inputs, grads)]
    rows = [[[p[1:] for p in parts] for parts in each] for each in lists]
    dec = (layers * (layers + 1) // 2, own[0], lists[1][0][0][0].shape[1])
    enc = (layers, own[1], lists[3][0][0][0].shape[1])
    arrays = [p[0] for each in lists for parts in each for p in parts] + [*early, *sums]
    arrays = [pltpu.with_memory_space_constraint(a, pltpu.VMEM) for a in arrays]
    return pl.pallas_call(
        functools.partial(grads_body, layers, scale, rows, own, late),
        name="grads",
        out_shape=[
            jax.ShapeDtypeStruct(dec, jnp.bfloat16),
            jax.ShapeDtypeStruct(enc, jnp.bfloat16),
            jax.ShapeDtypeStruct((layers, own[0]), jnp.float32),
        ],
        in_specs=inside(len(arrays)),
        out_specs=[pl.BlockSpec(memory_space=pltpu.HBM)] * 2 + inside(1),
        scratch_shapes=[
            pltpu.VMEM(dec, jnp.bfloat16),
            pltpu.VMEM(enc, jnp.bfloat16),
            pltpu.SemaphoreType.DMA((dec[0], dec[2] // piece(dec[2], 768))),
            pltpu.SemaphoreType.DMA((enc[0], enc[2] // piece(enc[2], 768))),
        ],
        compiler_params=pltpu.CompilerParams(vmem_limit_bytes=2 * (math.prod(dec) + math.prod(enc)) + 8 * MIB),
        cost_estimate=pl.CostEstimate(flops=0, bytes_accessed=0, transcendentals=0),
    )(*arrays)


def plain(acts_in, targets, enc_weight, bias, dec_weight, scale):
    layers, width, feats = enc_weight.shape
    feat, tok = lax.axis_size("feat"), lax.axis_size("tok")

    def gather(value):
        return lax.all_gather(value, "feat", axis=0, tiled=True)

    inputs, pre, codes, errors, grads, sums = [], [], [], [], [], []
    for g in range(tok):
        acts = swap(acts_in, "tok", g) if g else acts_in
        inputs.append([])
        pre.append([])
        codes.append([])
        for s in range(layers):
            inputs[g].append([gather(acts[:, s, :])])
            p, c = encode(s, inputs[g][s], enc_weight, bias, False)
            pre[g].append(p)
            codes[g].append(c)
    own = []
    for t in range(layers):
        halves = decode(t, range(t + 1), codes[0], dec_weight, layers, (), True, False)
        part = lax.psum_scatter(cat(halves), "feat", scatter_dimension=0, tiled=True)
        own.append((part.astype(jnp.float32) - targets[:, t, :].astype(jnp.float32)).astype(jnp.bfloat16))
    for g in range(tok):
        errors.append([[gather(swap(e, "tok", g) if g else e)] for e in own])
        d, total = back(errors[g], [[p] for p in pre[g]], dec_weight, layers, False)
        grads.append(d)
        sums.append(total)
    me = lax.axis_index("tok")
    index = me.reshape(1).astype(jnp.int32)

    def every(parts):
        return [[parts[g][s] for g in range(tok)] for s in range(layers)]

    def flat(parts):
        return [[parts[g][s][0] for g in range(tok)] for s in range(layers)]

    rows = feats // tok
    dec_out = dec_grads(every(codes), flat(errors), index, rows, scale, layers)
    enc_out = enc_grads(flat(inputs), every(grads), index, width // tok, scale, layers)
    total = sum(sums[1:], sums[0]).reshape(layers, feats) * scale
    return enc_out, lax.dynamic_slice_in_dim(total, me * rows, rows, axis=1), dec_out


def staged(acts_in, targets, enc_weight, bias, dec_weight, scale):
    layers, width, feats = enc_weight.shape
    n = acts_in.shape[0]
    quart = n * (lax.axis_size("feat") // 4)
    hop = quart // 2
    line = [4 * k for k in range(1, lax.axis_size("feat") // 4)]
    small = ((n, width), jnp.bfloat16)
    lows = [((quart, width), jnp.float32), ((quart, width), jnp.bfloat16)]

    def along(values):
        return [swap(v, "feat", bits) for v, bits in zip(values, line)]

    def across(value):
        return swap(value, "feat", 2)

    def core(value):
        return swap(value, "feat", 1)

    def away(value):
        return swap(value, "tok", 1)

    def encoded(s, parts, after=()):
        return encode(s, parts, enc_held, bias, True, after)

    def pair(keep, got, after):
        return local(pair_kernel, "pair", [keep, *got], lows, after)

    def error(low, got, ends, target, after):
        arrays = [low, got, *ends, target]
        return local(functools.partial(error_kernel, n), "error", arrays, [small], after)[0]

    def nears(parts):
        return [(p, 0, quart) for p in parts]

    def fars(parts):
        return [(p, quart, quart) for p in parts]

    def halves(value):
        return [(value, k * quart, quart) for k in (0, 2)], [(value, k * quart, quart) for k in (1, 3)]

    acts = [acts_in[:, 0, :]]
    ends = quart - n
    z_a0 = along([acts[0]] * len(line))
    enc_held = load([enc_weight])[0]
    acts.append(lax.optimization_barrier((acts_in, enc_held))[0][:, 1, :])
    done = [*z_a0, enc_held]
    line0, send, a1 = join([z_a0, [*z_a0, *acts], [acts[1]]], done)
    y_s, x_s = away(send), across(send)
    z_a1 = along([a1] * len(line))
    dec_held = load([dec_weight], [line0])[0]
    done = [*z_a1, x_s, y_s, dec_held]
    far0, far1 = [(x_s, ends, n), (x_s, 0, ends)], [(x_s, quart, n)]
    line1, col0 = join([z_a1, [acts[0], line0, *far0]], done)
    x_l1 = across(line1)
    in0 = [col0, core(col0)]
    pre0, code0 = encoded(0, in0)
    keep0, *give0 = decode(0, [0], [code0], dec_held, layers, (), True, True, (), 3)
    got0 = [core(g) for g in give0]
    done = [x_l1, *got0]
    low0, high0 = pair(keep0, got0, done)
    far1.append(x_l1)
    col1, far_both = join([[a1, line1, *far1], far0 + far1], [*done, high0])
    y_l1, x_h0 = away(line1), across(high0)
    in1 = [col1, core(col1)]
    early = decode(1, [0], [code0], dec_held, layers, (), False, True, (low0, col1))
    pre1, code1 = encoded(1, in1, early)
    keep1, *give1 = decode(1, [1], [code0, code1], dec_held, layers, early, True, True, (), 3)
    got1 = [core(g) for g in give1]
    done = [x_h0, y_l1, *got1]
    body = functools.partial(open_kernel, n, len(line))
    *ends0, low1, high1 = local(body, "open", [low0, x_h0, keep1, *got1], [small] * len(line) + lows, done)
    z_r0 = along(ends0)
    x_h1 = across(high1)
    done = [*z_r0, x_h1]
    target0, target1 = join([[targets[:, 0, :]], [targets[:, 1, :]]], [low1], 2 * quart * width * feats)
    arrays = [low0, x_h0, *z_r0, target0, low1, x_h1]
    shapes = [((2 * n, width), jnp.bfloat16)] * len(line) + [small]
    *turned, e0 = local(functools.partial(turn_kernel, n, len(line)), "turn", arrays, shapes, done)
    y_f, y_e0, x_e0 = away(far_both), away(e0), across(e0)
    z_t = along(turned)
    done = [*z_t, x_e0, y_e0, y_f]
    e1 = error(low1, x_h1, z_t, target1, done)
    lines = [(z, n, n) for z in z_t]
    near0, both = join([[e0, *lines], [*lines, e1]], done)
    there0 = [(y_s, ends, n), (y_s, 0, ends), (y_f, 0, quart)]
    there0, there1 = join([there0, [(y_s, quart, n), y_l1, (y_f, quart, quart)]], [*done, both])
    y_b, x_b = away(both), across(both)
    z_e1 = along([e1] * len(line))
    there_in0, there_in1 = [there0, core(there0)], [there1, core(there1)]
    there_pre0, there_code0 = encoded(0, there_in0)
    there_pre1, there_code1 = encoded(1, there_in1)
    done = [*z_e1, x_b, y_b, there_code0, there_code1]
    near1, send = join([[e1, *z_e1], z_e1], (), 32 * quart * width * feats)
    whole0, near_y0 = join(
        [[near0, x_e0, (x_b, 0, ends)], [y_e0, (y_b, 0, ends)]], [there_code0, there_code1]
    )
    y_g, x_g = away(send), across(send)
    err0 = [whole0, core(whole0)]
    near_err0 = [near_y0, core(near_y0)]
    first_own = first(err0, dec_held)
    first_near = first(near_err0, dec_held)
    share = (feats // lax.axis_size("tok"), width // lax.axis_size("tok"))
    early = ahead([code0] + halves(there_code0)[0], err0 + near_err0, share[0])
    done = [x_g, y_g, first_own, first_near]
    whole1, near_y1, go_x, go_y = join(
        [
            [near1, (x_b, ends, n), x_g],
            [(y_b, ends, n), y_g],
            [(near_y0, 0, hop), (y_b, ends, n), (y_g, 0, hop - n)],
            [(x_b, hop - n, quart - hop), (x_g, hop - n, quart - hop)],
        ],
        done,
    )
    y_t, x_o = away(go_y), across(go_x)
    err1 = [whole1, core(whole1)]
    near_err1 = [near_y1, core(near_y1)]

    near_pre, far_pre = zip(halves(there_pre0), halves(there_pre1))
    grad_own, sum_own = back([err0, err1], [[pre0], [pre1]], dec_held, layers, True, [first_own])
    grad_near, sum_near = back([near_err0, near_err1], near_pre, dec_held, layers, True, [first_near])
    done = [x_o, y_t, grad_own[0], grad_near[0], early]
    left = quart - hop
    far0, far1 = join([[(x_o, 0, hop), (y_t, 0, left)], [(x_o, hop, hop), (y_t, left, left)]], done)
    far_errs = [[far0, core(far0)], [far1, core(far1)]]
    early = [early, ahead([code0] + halves(there_code0)[0], err1 + near_err1, share[0], [far0])]
    grad_far, sum_far = back(far_errs, far_pre, dec_held, layers, True, (), early[1:])
    codes = [sum(halves(c), []) for c in (there_code0, there_code1)]
    seen = [nears(p) + fars(p) for p in (there_in0, there_in1)]
    dec_out, enc_out, bias_out = all_grads(
        [[code0] + codes[0], [code1] + codes[1]],
        [err0 + near_err0 + far_errs[0], err1 + near_err1 + far_errs[1]],
        [in0 + seen[0], in1 + seen[1]],
        [[grad_own[s], grad_near[s], grad_far[s]] for s in range(layers)],
        early,
        2,
        [sum_own, sum_near, sum_far],
        share,
        scale,
        layers,
    )
    return enc_out, bias_out, dec_out


def shards(acts_in, targets, enc_weight, enc_bias, dec_weight):
    layers, width, feats = enc_weight.shape
    n = acts_in.shape[0]
    feat, tok = lax.axis_size("feat"), lax.axis_size("tok")
    scale = 1.0 / math.sqrt(n * feat * tok)
    bias = enc_bias.reshape(layers, 1, feats)
    held = 2 * (math.prod(enc_weight.shape) + math.prod(dec_weight.shape))
    held += 4 * layers * n * feat * tok * (width + 2 * feats)
    fits = held <= 54 * MIB and n % 8 == 0 and (feats // tok) % 128 == 0 and (width // tok) % 128 == 0
    run = staged if fits and layers == 2 and tok == 2 and feat >= 8 else plain
    return run(acts_in, targets, enc_weight, bias, dec_weight, scale)


def solution(mesh):
    return jax.shard_map(
        shards,
        mesh=mesh,
        in_specs=(
            P(("tok", "feat"), None, None),
            P(("tok", "feat"), None, None),
            P(None, None, "feat"),
            P(None, "feat"),
            P(None, "feat", None),
        ),
        out_specs=(
            P(None, "tok", "feat"),
            P(None, ("feat", "tok")),
            P(None, ("feat", "tok"), None),
        ),
        check_vma=False,
    )
```
